256 devices in a mesh: expert: 64 (over z, y, core), mp: 4 (over x).
Axes of the slice: x: 4, y: 4, z: 8, core: 2. Of those that a mesh axis runs over, the one named last changes fastest.
Arguments:
- attn: bfloat16 [8192, 2048], P('expert', 'mp'), may hold values from -16 to 16
- out_proj: bfloat16 [2048, 2048], P('mp'), may hold values from -0.125 to 0.125
- tangent_proj: bfloat16 [2048, 2048], P('mp'), may hold values from -0.125 to 0.125
- resid: bfloat16 [8192, 2048], P('expert', 'mp'), may hold values from -6 to 6
- target: bfloat16 [8192, 2048], P('expert', 'mp'), may hold values from -6 to 6
- routes: int32 [8192, 2], P('expert'), may hold values from 0 to 63, all different within a row; in each aligned block of 128 rows (0 to 127, 128 to 255, ...) at most 5 rows name the same one
- gates: float32 [8192, 2], P('expert'), may hold values from 0.2 to 0.8
- w_gate: bfloat16 [64, 2048, 1408], P('expert', None, 'mp'), may hold values from -0.125 to 0.125
- w_up: bfloat16 [64, 2048, 1408], P('expert', None, 'mp'), may hold values from -0.125 to 0.125
- w_down: bfloat16 [64, 1408, 2048], P('expert', 'mp'), may hold values from -0.15625 to 0.15625
Outputs:
- hvp: float32 [4, 512, 2048], P('mp', 'expert')
The draws below stay inside these ranges and needn't reach their ends.
Inputs may be any that keep to these rules, and one draw needn't show every extreme that they name: `routes`: in each group of 128 rows held along one index of expert, no expert is named by more than 5 rows, a bound that some block reaches; the two experts of a row differ.
All inputs are finite; a program needn't handle non-finite values.
Results may differ from the reference program's by a relative error of at most 0.03.
Values may be sent and summed in bfloat16 or wider, within the bound.
A program may use at most 128 MiB of HBM per device.

```python
import math
import jax
import jax.numpy as jnp
import numpy as np
from jax import lax

D = 2048
FF = 1408
GROUP_TOK = 128
EXPERTS = 64
CAP = 5
TOKENS = 8192
N_EXPERT = 64
N_MP = 4


def strengthened(array, key, source, target, parts, factor):
    owner, partner = [(jnp.arange(array.shape[dim]) // (array.shape[dim] // parts)).reshape([-1 if axis == dim else 1 for axis in range(array.ndim)]) for dim in (source, target)]
    chosen = jax.random.permutation(key, parts)[partner]
    strong = (owner == chosen) | (owner == (partner + parts // 2) % parts)
    return jnp.where(strong, factor * array, array)


def levels(stream_key, shape, split, low, high):
    def one(axis_at, shards_of):
        draws = jax.random.uniform(jax.random.fold_in(jax.random.fold_in(stream_key, 6), axis_at), (shards_of,), jnp.float32, low / len(split), high / len(split))
        return jnp.repeat(jnp.exp(draws), shape[axis_at] // shards_of).reshape((-1,) + (1,) * (len(shape) - axis_at - 1))

    loudness = one(*split[0])
    for cut in split[1:]:
        loudness = loudness * one(*cut)
    return loudness


def assign_block(own_key, own, number, rows, count, top, reach, skew):
    ranking = jax.random.permutation(own_key, count)
    heavy_load, usual = portions_of(count, rows * top, reach, skew, True), portions_of(count, rows * top, reach, skew, False)
    places = jnp.arange(count)

    def named(sizes, rotation):
        used = int((sizes > 0).sum())
        fixed = max(1, used // 4)
        passed = fixed + (places - fixed + rotation * (used - fixed)) % max(1, count - fixed)
        return jnp.zeros((count,), jnp.int32).at[ranking[jnp.where(places < fixed, places, passed)]].set(jnp.asarray(sizes, jnp.int32))

    sizes = jnp.where(number % 4 == 0, named(heavy_load, number // 4), named(usual, number - number // 4 - 1))
    mixed = jax.random.permutation(jax.random.fold_in(own, 3), count)
    donor, receiver = mixed[0:count // 2 * 2:2], mixed[1:count // 2 * 2:2]
    room = jnp.minimum(sizes[donor] - 1, reach - sizes[receiver]) // 2
    room = jnp.where((donor == ranking[0]) | (receiver == ranking[0]) | (sizes[receiver] == 0), 0, jnp.maximum(room, 0))
    passed = jax.random.randint(jax.random.fold_in(own, 4), (count // 2,), 0, 1 << 20) % (room + 1)
    sizes = sizes.at[donor].add(-passed).at[receiver].add(passed)
    labels = jnp.searchsorted(jnp.cumsum(sizes), jnp.arange(rows * top), side="right").astype(jnp.int32)
    listing = labels.reshape(top, rows).T
    listing = listing[jax.random.permutation(jax.random.fold_in(own, 1), rows)]
    rotation = jax.random.randint(jax.random.fold_in(own, 2), (rows, 1), 0, top)
    return jnp.take_along_axis(listing, (jnp.arange(top)[None, :] + rotation) % top, axis=1)


def portions_of(count, total, reach, slope, full):
    loads = [(1 << 20) // math.isqrt(grade ** slope) + 1 for grade in range(1, count + 1)]
    largest = reach if full else min(reach, max(-(-total // count), total * loads[0] // sum(loads)))
    least = 1 if total - largest >= count - 1 else 0
    given, rest = [largest] + [least] * (count - 1), total - largest - least * (count - 1)
    while rest > 0:
        movable = [i for i in range(1, count) if given[i] < largest] or [i for i in range(1, count) if given[i] < reach]
        whole, budget = sum([loads[i] for i in movable]), rest
        for i in movable:
            extra = min(reach - given[i], max(1, budget * loads[i] // whole), rest)
            given[i] = given[i] + extra
            rest = rest - extra
    return np.array(given)


def scatter_about(rng, shape, width, bound, shards=(), kind=jnp.bfloat16):
    factor_of = levels(rng, shape, shards, -0.22, 0.18) if shards else 1.0
    values = jax.random.normal(rng, shape, jnp.float32) * width * factor_of
    return jnp.minimum(jnp.maximum(values, -bound), bound).astype(kind)


def heavy_noise(stream_key, dims, width, reach, shards, heavy, held_as=jnp.bfloat16):
    drawn = width * jax.random.normal(stream_key, dims, jnp.float32)
    if shards:
        drawn = drawn * levels(stream_key, dims, shards, -0.22, 0.18)
    return jnp.clip(strengthened(drawn, jax.random.fold_in(stream_key, 3), *heavy), -reach, reach).astype(held_as)


def setup_inputs(seed: int = 0) -> dict:
    seeds = jax.random.split(jax.random.key(seed), 11)
    attn = heavy_noise(seeds[0], (TOKENS, D), 1.0, 16.0, ((0, 64), (1, 4)), (0, 1, 64, 4.0))
    out_proj = scatter_about(seeds[1], (D, D), D ** -0.5, 0.125, ((0, 4),))
    tangent_proj = scatter_about(seeds[2], (D, D), D ** -0.5, 0.125, ((0, 4),))
    resid = scatter_about(seeds[3], (TOKENS, D), 1.0, 6.0, ((0, 64), (1, 4)))
    target = scatter_about(seeds[4], (TOKENS, D), 1.0, 6.0, ((0, 64), (1, 4)))
    routes_keys = jax.random.split(jax.random.fold_in(seeds[5], 1), TOKENS // GROUP_TOK)
    routes_turns = jax.random.permutation(jax.random.fold_in(seeds[5], 3), TOKENS // GROUP_TOK)
    routes = jax.vmap(lambda own, number: assign_block(jax.random.fold_in(seeds[5], 2), own, number, GROUP_TOK, EXPERTS, 2, CAP, 2))(routes_keys, routes_turns).reshape((TOKENS, 2))
    gates = jnp.clip(0.2 + 0.6 * jax.random.uniform(seeds[6], (TOKENS, 2), jnp.float32) ** levels(seeds[6], (TOKENS, 2), ((0, 64),), -0.2, 0.2), 0.2, 0.8)
    w_gate = scatter_about(seeds[7], (EXPERTS, D, FF), D ** -0.5, 0.125, ((0, 64), (2, 4)))
    w_up = scatter_about(seeds[8], (EXPERTS, D, FF), D ** -0.5, 0.125, ((0, 64), (2, 4)))
    w_down = scatter_about(seeds[9], (EXPERTS, FF, D), FF ** -0.5, 0.15625, ((0, 64), (1, 4)))
    return {"attn": attn, "out_proj": out_proj, "tangent_proj": tangent_proj, "resid": resid, "target": target, "routes": routes, "gates": gates, "w_gate": w_gate, "w_up": w_up, "w_down": w_down}


def rounded(values):
    return lax.optimization_barrier(values.astype(jnp.bfloat16)).astype(jnp.float32)

def silu_terms(gate_pre):
    sigma = jax.nn.sigmoid(gate_pre)
    silu_val = gate_pre * sigma
    silu_one = sigma * (1.0 + gate_pre * (1.0 - sigma))
    silu_two = sigma * (1.0 - sigma) * (2.0 + gate_pre * (1.0 - 2.0 * sigma))
    return (silu_val, silu_one, silu_two)

def pre_acts(inputs, inputs_tan, gate_w, up_w):
    gate_pre = jnp.dot(inputs, gate_w, preferred_element_type=jnp.float32)
    up_pre = jnp.dot(inputs, up_w, preferred_element_type=jnp.float32)
    gate_tan = jnp.dot(inputs_tan, gate_w, preferred_element_type=jnp.float32)
    up_tan = jnp.dot(inputs_tan, up_w, preferred_element_type=jnp.float32)
    return (gate_pre, up_pre, gate_tan, up_tan)

def reference(attn, out_proj, tangent_proj, resid, target, routes, gates, w_gate, w_up, w_down):
    quarter = D // N_MP
    hidden_part = FF // N_MP
    z_val = jnp.zeros((TOKENS, D), jnp.float32)
    z_tan = jnp.zeros((TOKENS, D), jnp.float32)
    for block in range(N_MP):
        cols = attn[:, block * quarter:(block + 1) * quarter]
        z_val = z_val + rounded(jnp.dot(cols, out_proj[block * quarter:(block + 1) * quarter], preferred_element_type=jnp.float32))
        z_tan = z_tan + rounded(jnp.dot(cols, tangent_proj[block * quarter:(block + 1) * quarter], preferred_element_type=jnp.float32))
    x_val = (resid.astype(jnp.float32) + z_val).astype(jnp.bfloat16)
    x_tan = z_tan.astype(jnp.bfloat16)
    slots_per = N_EXPERT * CAP
    flat_ids = routes.reshape(-1).astype(jnp.int32)
    count = flat_ids.shape[0]
    onehot = (flat_ids[:, None] == jnp.arange(EXPERTS, dtype=jnp.int32)[None, :]).astype(jnp.int32)
    position = lax.optimization_barrier(jnp.sum(jnp.cumsum(onehot, axis=0) * onehot, axis=1)) - 1
    slot_index = (flat_ids * slots_per + position).astype(jnp.int32)
    numbers = jnp.arange(count, dtype=jnp.int32)
    source = jnp.zeros((EXPERTS * slots_per,), jnp.int32).at[slot_index].set(numbers // 2)
    filled = jnp.zeros((EXPERTS * slots_per,), jnp.bool_).at[slot_index].set(True)
    slot_gate = jnp.zeros((EXPERTS * slots_per,), jnp.float32).at[slot_index].set(gates.reshape(-1).astype(jnp.float32))

    def spread(values):
        taken = jnp.where(filled[:, None], values[source], jnp.zeros((), values.dtype))
        return taken.reshape(EXPERTS, slots_per, values.shape[1])

    def forward(items):
        inputs, inputs_tan, gate_w, up_w, down_w = items
        gate_pre, up_pre, gate_tan, up_tan = pre_acts(inputs, inputs_tan, gate_w, up_w)
        silu_val, silu_one, silu_two = silu_terms(gate_pre)
        hidden = (silu_val * up_pre).astype(jnp.bfloat16)
        hidden_tan = (silu_one * gate_tan * up_pre + silu_val * up_tan).astype(jnp.bfloat16)
        out_row = jnp.zeros((inputs.shape[0], D), jnp.float32)
        out_tan = jnp.zeros((inputs.shape[0], D), jnp.float32)
        for block in range(N_MP):
            lower = block * hidden_part
            upper = lower + hidden_part
            out_row = out_row + rounded(jnp.dot(hidden[:, lower:upper], down_w[lower:upper], preferred_element_type=jnp.float32))
            out_tan = out_tan + rounded(jnp.dot(hidden_tan[:, lower:upper], down_w[lower:upper], preferred_element_type=jnp.float32))
        return (out_row.astype(jnp.bfloat16), out_tan.astype(jnp.bfloat16))
    out_all, out_tan_all = lax.map(forward, (spread(x_val), spread(x_tan), w_gate, w_up, w_down))

    def combine(values):
        picked = values.reshape(EXPERTS * slots_per, D)[slot_index].astype(jnp.float32).reshape(TOKENS, 2, D)
        return lax.optimization_barrier(jnp.sum(gates.astype(jnp.float32)[:, :, None] * picked, axis=1))
    y_val = x_val.astype(jnp.float32) + combine(out_all)
    y_tan = x_tan.astype(jnp.float32) + combine(out_tan_all)
    diff = y_val - target.astype(jnp.float32)

    def weighted(values):
        taken = (slot_gate[:, None] * values[source]).astype(jnp.bfloat16)
        return taken.reshape(EXPERTS, slots_per, D)

    def backward(items):
        inputs, inputs_tan, cot, cot_tan, gate_w, up_w, down_w = items
        gate_pre, up_pre, gate_tan, up_tan = pre_acts(inputs, inputs_tan, gate_w, up_w)
        silu_val, silu_one, silu_two = silu_terms(gate_pre)
        back_tan = jnp.zeros((inputs.shape[0], D), jnp.float32)
        for block in range(N_MP):
            lower = block * hidden_part
            upper = lower + hidden_part
            down_part = down_w[lower:upper]
            grad_h = jnp.dot(cot, down_part.T, preferred_element_type=jnp.float32)
            grad_h_tan = jnp.dot(cot_tan, down_part.T, preferred_element_type=jnp.float32)
            sv = silu_val[:, lower:upper]
            so = silu_one[:, lower:upper]
            st = silu_two[:, lower:upper]
            up_b = up_pre[:, lower:upper]
            up_bt = up_tan[:, lower:upper]
            gate_bt = gate_tan[:, lower:upper]
            da_tan = ((grad_h_tan * up_b + grad_h * up_bt) * so + grad_h * up_b * st * gate_bt).astype(jnp.bfloat16)
            db_tan = (grad_h_tan * sv + grad_h * so * gate_bt).astype(jnp.bfloat16)
            term = jnp.dot(da_tan, gate_w[:, lower:upper].T, preferred_element_type=jnp.float32)
            term = term + jnp.dot(db_tan, up_w[:, lower:upper].T, preferred_element_type=jnp.float32)
            back_tan = back_tan + rounded(term)
        return back_tan.astype(jnp.bfloat16)
    back_all = lax.map(backward, (spread(x_val), spread(x_tan), weighted(diff), weighted(y_tan), w_gate, w_up, w_down))
    dx_tan = (y_tan + combine(back_all)).astype(jnp.bfloat16)
    hvp_full = jnp.dot(attn.T, dx_tan, preferred_element_type=jnp.float32) / math.sqrt(TOKENS)
    return hvp_full.reshape(N_MP, D // N_MP, D)
```

```python
import functools
import math

import jax
import jax.numpy as jnp
from jax import lax
from jax.experimental import pallas as pl
from jax.experimental.pallas import tpu as pltpu
from jax.sharding import PartitionSpec as P

MESH = pl.DeviceIdType.MESH
BF = jnp.bfloat16
F32 = jnp.float32
N_MP = 4
N_CORE = 2
CHUNKS = 2
BACK_CHUNKS = 2


class Names:
    def __init__(self):
        self.names, self.shapes = [], []

    def add(self, name, shape):
        self.names.append(name)
        self.shapes.append(shape)

    def bind(self, refs):
        for name, ref in zip(self.names, refs, strict=True):
            setattr(self, name, ref)


def dot(left, right):
    return jnp.dot(left, right, preferred_element_type=F32)


def dot_last(left, right):
    return lax.dot_general(left, right, (((1,), (1,)), ((), ())), preferred_element_type=F32)


def dot_first(left, right):
    return lax.dot_general(left, right, (((0,), (0,)), ((), ())), preferred_element_type=F32)


def silu_terms(gate_pre):
    sigma = jax.nn.sigmoid(gate_pre)
    silu_val = gate_pre * sigma
    silu_one = sigma * (1.0 + gate_pre * (1.0 - sigma))
    silu_two = sigma * (1.0 - sigma) * (2.0 + gate_pre * (1.0 - 2.0 * sigma))
    return (silu_val, silu_one, silu_two)


def each(lower, upper, body):
    def step(i, carry):
        body(i)
        return carry

    lax.fori_loop(lower, upper, step, 0)


def pipeline(stages, chunks):
    for turn in range(len(stages) + chunks - 1):
        for k in range(chunks):
            if 0 <= turn - k < len(stages):
                stages[turn - k](k)


class Exchange:
    def __init__(self, src, dst, sems, n, me, device):
        self.src, self.dst, self.n, self.me, self.device = src, dst, n, me, device
        self.ssem, self.rsem = sems

    def copy(self, k, d, block, landing, device):
        return pltpu.make_async_remote_copy(
            src_ref=self.src.at[k, block],
            dst_ref=self.dst.at[k, landing],
            send_sem=self.ssem.at[k, d],
            recv_sem=self.rsem.at[k, d],
            device_id=device,
            device_id_type=MESH,
        )

    def out(self, k, d):
        to = lax.rem(self.me + d, self.n)
        return self.copy(k, d, to, self.me, self.device(to))

    def start(self, k):
        each(1, self.n, lambda d: self.out(k, d).start())
        self.dst[k, pl.ds(self.me, 1)] = self.src[k, pl.ds(self.me, 1)]

    def wait(self, k):
        def body(d):
            source = lax.rem(self.me + self.n - d, self.n)
            self.copy(k, d, source, source, self.device(source)).wait_recv()

        each(1, self.n, body)

    def drain(self, k):
        each(1, self.n, lambda d: self.out(k, d).wait_send())


class Ring:
    def __init__(self):
        self.expert = lax.axis_index("expert")
        self.me = lax.axis_index("mp")
        self.right = lax.rem(self.me + 1, N_MP)
        self.left = lax.rem(self.me + N_MP - 1, N_MP)
        self.opp = lax.rem(self.me + 2, N_MP)

    def copy(self, src, dst, ssem, rsem, to):
        return pltpu.make_async_remote_copy(
            src_ref=src,
            dst_ref=dst,
            send_sem=ssem,
            recv_sem=rsem,
            device_id=(self.expert, to),
            device_id_type=MESH,
        )


class Scatter:
    def __init__(self, ring, part, hop, total, sems, rows):
        self.ring, self.part, self.hop, self.total, self.rows = ring, part, hop, total, rows
        self.ssem, self.rsem = sems
        self.half = rows // 2

    def copy(self, k, i):
        r, h = self.ring, self.half
        first, second = pl.ds(0, h), pl.ds(h, h)
        part, hop, total = self.part.at[k], self.hop.at[k], self.total.at[k]
        plan = (
            (part.at[r.opp, first], hop.at[0], r.left),
            (part.at[r.opp, second], hop.at[1], r.right),
            (part.at[r.left, second], total.at[0, second], r.left),
            (part.at[r.right, first], total.at[1, first], r.right),
            (part.at[r.left, first], total.at[0, first], r.left),
            (part.at[r.right, second], total.at[1, second], r.right),
        )
        src, dst, to = plan[i]
        return r.copy(src, dst, self.ssem.at[k, i], self.rsem.at[k, i], to)

    def start(self, k, index):
        self.copy(k, index).start()

    def middle(self, k):
        r, h = self.ring, self.half
        self.copy(k, 0).wait_recv()
        self.add(k, r.left, pl.ds(0, h), 0)
        self.copy(k, 4).start()
        self.copy(k, 1).wait_recv()
        self.add(k, r.right, pl.ds(h, h), 1)
        self.copy(k, 5).start()

    def add(self, k, block, rows, side):
        value = self.part[k, pl.ds(block, 1), rows, :][0].astype(F32) + self.hop[k, side].astype(F32)
        self.part[k, pl.ds(block, 1), rows, :] = value.astype(BF)[None]

    def finish(self, k):
        for i in (2, 3, 4, 5):
            self.copy(k, i).wait_recv()
        own = self.part[k, pl.ds(self.ring.me, 1)][0].astype(F32)
        return own + self.total[k, 0].astype(F32) + self.total[k, 1].astype(F32)

    def drain(self, k):
        for i in range(6):
            self.copy(k, i).wait_send()


class Gather:
    def __init__(self, ring, full, sems, rows):
        self.ring, self.full = ring, full
        self.ssem, self.rsem = sems
        self.half = rows // 2

    def move(self, k, i, block, rows, to):
        ref = self.full.at[k, block, rows]
        return self.ring.copy(ref, ref, self.ssem.at[k, i], self.rsem.at[k, i], to)

    def copy(self, k, i):
        r, h = self.ring, self.half
        first, second = pl.ds(0, h), pl.ds(h, h)
        plan = (
            (r.me, first, r.left),
            (r.me, second, r.right),
            (r.me, second, r.left),
            (r.me, first, r.right),
            (r.right, first, r.left),
            (r.left, second, r.right),
        )
        return self.move(k, i, *plan[i])

    def arrival(self, k, i):
        r, h = self.ring, self.half
        first, second = pl.ds(0, h), pl.ds(h, h)
        plan = (
            (r.right, first),
            (r.left, second),
            (r.right, second),
            (r.left, first),
            (r.opp, first),
            (r.opp, second),
        )
        return self.move(k, i, *plan[i], r.left)

    def start(self, k):
        for i in range(4):
            self.copy(k, i).start()

    def middle(self, k):
        for i in range(2):
            self.arrival(k, i).wait_recv()
            self.copy(k, 4 + i).start()

    def finish(self, k):
        for i in range(2, 6):
            self.arrival(k, i).wait_recv()

    def drain(self, k):
        for i in range(6):
            self.copy(k, i).wait_send()


def iota(shape, dim):
    return lax.broadcasted_iota(jnp.int32, shape, dim)


def kernel(sizes, names, *refs):
    (attn_h, out_proj_h, tan_proj_h, resid, target, pick, back0, back1, slot_gate, gates) = refs[:10]
    w_gate_h, w_up_h, w_down_h, out = refs[10:14]
    s = names
    s.bind(refs[14:])
    nz, nyc, cap, tokens, quarter, hidden, chunks, back_chunks = sizes
    ny = nyc // N_CORE
    cw = quarter // chunks
    bw = quarter // 2 // back_chunks
    half = nz * cap
    block = 2 * half
    rows = nyc * block
    model = N_MP * quarter

    ring = Ring()
    me_e, me_m = ring.expert, ring.me
    z, yc = lax.div(me_e, nyc), lax.rem(me_e, nyc)
    y, core = lax.div(yc, N_CORE), lax.rem(yc, N_CORE)

    def at_z(to):
        return (to * nyc + yc, me_m)

    def at_yc(to):
        return (z * nyc + to, me_m)

    loads = [
        pltpu.make_async_copy(src, dst, s.load_sem.at[i])
        for i, (src, dst) in enumerate(
            (
                (attn_h, s.attn),
                (out_proj_h, s.out_proj),
                (tan_proj_h, s.tan_proj),
                (w_gate_h.at[0], s.w_gate),
                (w_up_h.at[0], s.w_up),
                (w_down_h.at[0], s.w_down),
            )
        )
    ]
    for load in loads:
        load.start()

    barrier = pltpu.get_barrier_semaphore()

    def greet(device):
        pl.semaphore_signal(barrier, inc=1, device_id=device, device_id_type=MESH)

    each(1, nz, lambda d: greet(at_z(lax.rem(z + d, nz))))
    each(1, nyc, lambda d: greet(at_yc(lax.rem(yc + d, nyc))))
    each(1, N_MP, lambda d: greet((me_e, lax.rem(me_m + d, N_MP))))
    pl.semaphore_wait(barrier, nz + nyc + N_MP - 3)

    def sems(name):
        return getattr(s, name + "_ssem"), getattr(s, name + "_rsem")

    scat_z = Scatter(ring, s.part_z, s.hop_z, s.total_z, sems("scat_z"), 2 * tokens)
    go_z = Exchange(s.go_a, s.go_b, sems("go_z"), nz, z, at_z)
    go_yc = Exchange(s.go_c, s.go_d, sems("go_yc"), nyc, yc, at_yc)
    gather_x = Gather(ring, s.x_full, sems("gather_x"), rows)
    scat_o = Scatter(ring, s.part_o, s.hop_o, s.total_o, sems("scat_o"), rows)
    ret_yc = Exchange(s.ret_a, s.ret_b, sems("ret_yc"), nyc, yc, at_yc)
    ret_z = Exchange(s.ret_c, s.ret_d, sems("ret_z"), nz, z, at_z)
    cot_z = Exchange(s.cot_a, s.cot_b, sems("cot_z"), nz, z, at_z)
    cot_yc = Exchange(s.cot_c, s.cot_d, sems("cot_yc"), nyc, yc, at_yc)
    gather_c = Gather(ring, s.c_full, sems("gather_c"), rows)
    scat_b = Scatter(ring, s.part_b, s.hop_b, s.total_b, sems("scat_b"), rows)
    bak_yc = Exchange(s.bak_a, s.bak_b, sems("bak_yc"), nyc, yc, at_yc)
    bak_z = Exchange(s.bak_c, s.bak_d, sems("bak_z"), nz, z, at_z)
    gather_a = Gather(ring, s.attn_full, sems("gather_a"), tokens)

    def swap(src, dst, k, width):
        value = dot(s.swap[...], src[k].reshape(rows, width))
        dst[k] = value.astype(BF).reshape(nyc, block, width)

    loads[0].wait()
    loads[1].wait()
    loads[2].wait()

    def z_part(k, q):
        columns = pl.ds(pl.multiple_of(q * quarter + k * cw, 128), cw)
        s.part_z[k, pl.ds(q, 1), pl.ds(0, tokens), :] = dot(s.attn[...], s.out_proj[:, columns]).astype(BF)[None]
        s.part_z[k, pl.ds(q, 1), pl.ds(tokens, tokens), :] = dot(s.attn[...], s.tan_proj[:, columns]).astype(BF)[None]

    def z_start(k):
        z_part(k, ring.opp)
        scat_z.start(k, 0)
        scat_z.start(k, 1)
        z_part(k, ring.left)
        scat_z.start(k, 2)
        z_part(k, ring.right)
        scat_z.start(k, 3)
        z_part(k, ring.me)

    def spread_x(k):
        if k == 0:
            r = iota((rows, 1), 0)
            a, h, b, p = r // block, (r % block) // half, (r % half) // cap, r % cap
            s.swap[...] = (iota((rows, rows), 1) == b * block + h * half + a * cap + p).astype(F32).astype(BF)
        value = scat_z.finish(k)
        columns = pl.ds(k * cw, cw)
        s.x_in[k, pl.ds(0, tokens), :] = (
            resid[:, columns].astype(F32) + value[:tokens]
        ).astype(BF)
        s.x_in[k, pl.ds(tokens, tokens), :] = value[tokens:].astype(BF)
        s.go_a[k] = dot(pick[...], s.x_in[k]).astype(BF).reshape(nz, block, cw)
        go_z.start(k)

    def pass_x(k):
        go_z.wait(k)
        swap(s.go_b, s.go_c, k, cw)
        go_yc.start(k)

    def gather_start_x(k):
        go_yc.wait(k)
        s.x_full[k, pl.ds(me_m, 1)] = s.go_d[k].reshape(1, rows, cw)
        gather_x.start(k)

    step_rows = 2 * block

    def pre_acts(k):
        gather_x.finish(k)
        if k == 0:
            loads[3].wait()
            loads[4].wait()

        def body(i):
            at = pl.ds(pl.multiple_of(i * step_rows, step_rows), step_rows)
            gate = jnp.zeros((step_rows, hidden), F32)
            up = jnp.zeros((step_rows, hidden), F32)
            for m in range(N_MP):
                features = pl.ds(m * quarter + k * cw, cw)
                values = s.x_full[k, m, at, :]
                gate = gate + dot(values, s.w_gate[features, :])
                up = up + dot(values, s.w_up[features, :])
            if k:
                gate = gate + s.gate[at, :]
                up = up + s.up[at, :]
            s.gate[at, :] = gate
            s.up[at, :] = up

        each(0, rows // step_rows, body)

    def permute_attn():
        r = iota((1, quarter), 1)
        per = quarter // (nz * nyc)
        c, yy, zz, p = (
            r // (quarter // N_CORE),
            (r // (nz * per)) % ny,
            (r // per) % nz,
            r % per,
        )
        wanted = ((zz * ny + yy) * N_CORE + c) * per + p
        permute = (iota((quarter, quarter), 0) == wanted).astype(F32).astype(BF)
        s.attn_full[0, pl.ds(me_m, 1)] = dot(s.attn[...], permute).astype(BF)[None]

    def attn_start(k):
        if k == chunks - 1:
            permute_attn()
            gather_a.start(0)

    pipeline(
        (
            z_start,
            scat_z.middle,
            spread_x,
            attn_start,
            pass_x,
            gather_start_x,
            gather_x.middle,
            pre_acts,
        ),
        chunks,
    )
    gather_a.middle(0)

    def activations(i):
        at, tan_at = pl.ds(pl.multiple_of(i * block, 8), half), pl.ds(pl.multiple_of(i * block + half, 8), half)
        gate_pre, gate_tan = s.gate[at, :], s.gate[tan_at, :]
        up_pre, up_tan = s.up[at, :], s.up[tan_at, :]
        silu_val, silu_one, _ = silu_terms(gate_pre)
        hid = silu_val * up_pre
        hid_tan = silu_one * gate_tan * up_pre + silu_val * up_tan
        s.hidden[pl.ds(pl.multiple_of(i * block, 16), block), :] = jnp.concatenate([hid, hid_tan], 0).astype(BF)

    each(0, nyc, activations)
    loads[5].wait()

    def o_part(k, q):
        columns = pl.ds(pl.multiple_of(q * quarter + k * cw, 128), cw)
        s.part_o[k, pl.ds(q, 1)] = dot(s.hidden[...], s.w_down[:, columns]).astype(BF)[None]

    def o_start(k):
        o_part(k, ring.opp)
        scat_o.start(k, 0)
        scat_o.start(k, 1)
        o_part(k, ring.left)
        scat_o.start(k, 2)
        o_part(k, ring.right)
        scat_o.start(k, 3)
        o_part(k, ring.me)

    def return_o(k):
        s.ret_a[k] = scat_o.finish(k).astype(BF).reshape(nyc, block, cw)
        ret_yc.start(k)

    def pass_o(k):
        ret_yc.wait(k)
        swap(s.ret_b, s.ret_c, k, cw)
        ret_z.start(k)

    def combine(values):
        return gates[:, 0:1] * dot(back0[...], values) + gates[:, 1:2] * dot(back1[...], values)

    def residual(k):
        ret_z.wait(k)
        columns = pl.ds(k * cw, cw)
        both = s.x_in[k].astype(F32) + combine(s.ret_d[k].reshape(rows, cw))
        s.y_tan[:, columns] = both[tokens:]
        diff = both[:tokens] - target[:, columns].astype(F32)
        sent = jnp.concatenate([diff, both[tokens:]], 0).astype(BF)
        s.cot_a[k] = (dot(pick[...], sent) * slot_gate[...]).astype(BF).reshape(nz, block, cw)
        cot_z.start(k)

    def pass_c(k):
        cot_z.wait(k)
        swap(s.cot_b, s.cot_c, k, cw)
        cot_yc.start(k)

    def gather_start_c(k):
        cot_yc.wait(k)
        s.c_full[k, pl.ds(me_m, 1)] = s.cot_d[k].reshape(1, rows, cw)
        gather_c.start(k)

    def grad_hidden(k):
        gather_c.finish(k)

        def body(i):
            at = pl.ds(pl.multiple_of(i * step_rows, step_rows), step_rows)
            grad = jnp.zeros((step_rows, hidden), F32)
            for m in range(N_MP):
                features = pl.ds(m * quarter + k * cw, cw)
                grad = grad + dot_last(s.c_full[k, m, at, :], s.w_down[:, features])
            if k:
                grad = grad + s.grad[at, :]
            s.grad[at, :] = grad

        each(0, rows // step_rows, body)

    pipeline(
        (
            o_start,
            scat_o.middle,
            return_o,
            pass_o,
            residual,
            pass_c,
            gather_start_c,
            gather_c.middle,
            grad_hidden,
        ),
        chunks,
    )

    def tangents(i):
        at, tan_at = pl.ds(pl.multiple_of(i * block, 8), half), pl.ds(pl.multiple_of(i * block + half, 8), half)
        gate_pre, gate_tan = s.gate[at, :], s.gate[tan_at, :]
        up_pre, up_tan = s.up[at, :], s.up[tan_at, :]
        dh, dh_tan = s.grad[at, :], s.grad[tan_at, :]
        silu_val, silu_one, silu_two = silu_terms(gate_pre)
        da_tan = (dh_tan * up_pre + dh * up_tan) * silu_one + dh * up_pre * silu_two * gate_tan
        db_tan = dh_tan * silu_val + dh * silu_one * gate_tan
        to = pl.ds(pl.multiple_of(i * half, 8), half)
        s.da_tan[to, :] = da_tan
        s.db_tan[to, :] = db_tan

    each(0, nyc, tangents)

    def b_part(k, q):
        da_tan, db_tan = s.da_tan[...].astype(BF), s.db_tan[...].astype(BF)
        sides = []
        for h in range(2):
            features = pl.ds(pl.multiple_of(q * quarter + h * (quarter // 2) + k * bw, 128), bw)
            term = dot_last(da_tan, s.w_gate[features, :]) + dot_last(db_tan, s.w_up[features, :])
            sides.append(term.reshape(nyc, half, bw))
        s.part_b[k, pl.ds(q, 1)] = jnp.concatenate(sides, 1).astype(BF).reshape(1, rows, bw)

    def b_start(k):
        b_part(k, ring.opp)
        scat_b.start(k, 0)
        scat_b.start(k, 1)
        b_part(k, ring.left)
        scat_b.start(k, 2)
        b_part(k, ring.right)
        scat_b.start(k, 3)
        b_part(k, ring.me)

    def return_b(k):
        s.bak_a[k] = scat_b.finish(k).astype(BF).reshape(nyc, block, bw)
        bak_yc.start(k)

    def pass_b(k):
        bak_yc.wait(k)
        swap(s.bak_b, s.bak_c, k, bw)
        bak_z.start(k)

    def grad_in(k):
        bak_z.wait(k)
        both = combine(s.bak_d[k].reshape(rows, bw))
        for h in range(2):
            columns = pl.ds(h * (quarter // 2) + k * bw, bw)
            s.dx[:, columns] = (s.y_tan[:, columns] + both[h * tokens : (h + 1) * tokens]).astype(BF)

    pipeline((b_start, scat_b.middle, return_b, pass_b, grad_in), back_chunks)
    gather_a.finish(0)

    per = quarter // (nz * nyc)
    run = nz * per

    def products(c):
        for m in range(N_MP):
            columns = pl.ds(pl.multiple_of(c * (quarter // N_CORE), 128), quarter // N_CORE)
            value = dot_first(s.attn_full[0, m, :, columns], s.dx[...]).astype(BF)
            s.prod[pl.ds(c, 1), :, pl.ds(m * run, run), :] = value.reshape(1, ny, run, quarter)

    other = 1 - core

    def core_copy():
        return pltpu.make_async_remote_copy(
            src_ref=s.prod.at[other],
            dst_ref=s.core_in,
            send_sem=s.core_ssem,
            recv_sem=s.core_rsem,
            device_id=at_yc(y * N_CORE + other),
            device_id_type=MESH,
        )

    products(other)
    core_copy().start()
    products(core)
    core_copy().wait_recv()

    def add_core(i):
        value = s.prod[pl.ds(core, 1), pl.ds(i, 1)].astype(F32)[0] + s.core_in[pl.ds(i, 1)].astype(F32)
        s.sum_y[0, pl.ds(i, 1)] = value.astype(BF)

    each(0, ny, add_core)
    ex_y = Exchange(s.sum_y, s.in_y, sems("ex_y"), ny, y, lambda to: at_yc(to * N_CORE + core))
    ex_z = Exchange(s.sum_z, s.in_z, sems("ex_z"), nz, z, at_z)
    ex_y.start(0)
    ex_y.wait(0)
    total = jnp.sum(s.in_y[0].astype(F32), axis=0)
    total = total.reshape(N_MP, nz, per, quarter)
    total = jnp.stack([total[m] for m in range(N_MP)], 1)
    s.sum_z[0] = total.reshape(nz, N_MP * per, quarter).astype(BF)
    ex_z.start(0)
    ex_z.wait(0)
    total = jnp.sum(s.in_z[0].astype(F32), axis=0)
    s.last_a[0] = (total * (1.0 / math.sqrt(tokens * nz * nyc))).reshape(N_MP, per, quarter)
    last = Exchange(s.last_a, s.last_b, sems("last"), N_MP, me_m, lambda to: (me_e, to))
    last.start(0)
    last.wait(0)
    for m in range(N_MP):
        out[0, :, m * quarter : (m + 1) * quarter] = s.last_b[0, m]

    for k in range(chunks):
        for stage in (scat_z, go_z, go_yc, gather_x, scat_o, ret_yc, ret_z, cot_z, cot_yc, gather_c):
            stage.drain(k)
    for k in range(back_chunks):
        for stage in (scat_b, bak_yc, bak_z):
            stage.drain(k)
    gather_a.drain(0)
    core_copy().wait_send()
    ex_y.drain(0)
    ex_z.drain(0)
    last.drain(0)


def scratch(sizes):
    nz, nyc, cap, tokens, quarter, hidden, chunks, back_chunks = sizes
    ny = nyc // N_CORE
    cw, bw = quarter // chunks, quarter // 2 // back_chunks
    block = 2 * nz * cap
    rows = nyc * block
    model = N_MP * quarter
    per = quarter // (nz * nyc)
    names = Names()

    def vmem(name, shape, kind=BF):
        names.add(name, pltpu.VMEM(shape, kind))

    def sems(name, k, n):
        names.add(name + "_ssem", pltpu.SemaphoreType.DMA((k, n)))
        names.add(name + "_rsem", pltpu.SemaphoreType.DMA((k, n)))

    names.add("load_sem", pltpu.SemaphoreType.DMA((6,)))
    vmem("attn", (tokens, quarter))
    vmem("out_proj", (quarter, model))
    vmem("tan_proj", (quarter, model))
    vmem("w_gate", (model, hidden))
    vmem("w_up", (model, hidden))
    vmem("w_down", (hidden, model))
    vmem("swap", (rows, rows))
    for tag, count, height, width in (
        ("z", chunks, 2 * tokens, cw),
        ("o", chunks, rows, cw),
        ("b", back_chunks, rows, bw),
    ):
        vmem("part_" + tag, (count, N_MP, height, width))
        vmem("hop_" + tag, (count, 2, height // 2, width))
        vmem("total_" + tag, (count, 2, height, width))
        sems("scat_" + tag, count, 6)
    for tag, count, width in (("go", chunks, cw), ("ret", chunks, cw), ("cot", chunks, cw), ("bak", back_chunks, bw)):
        for letter in "abcd":
            vmem(f"{tag}_{letter}", (count, nz, block, width))
        sems(tag + "_z", count, nz)
        sems(tag + "_yc", count, nyc)
    for tag in "xc":
        vmem(tag + "_full", (chunks, N_MP, rows, cw))
        sems("gather_" + tag, chunks, 6)
    vmem("attn_full", (1, N_MP, tokens, quarter))
    sems("gather_a", 1, 6)
    vmem("x_in", (chunks, 2 * tokens, cw))
    vmem("gate", (rows, hidden), F32)
    vmem("up", (rows, hidden), F32)
    vmem("grad", (rows, hidden), F32)
    vmem("hidden", (rows, hidden))
    vmem("da_tan", (rows // 2, hidden), F32)
    vmem("db_tan", (rows // 2, hidden), F32)
    vmem("y_tan", (tokens, quarter), F32)
    vmem("dx", (tokens, quarter))
    run = N_MP * nz * per
    vmem("prod", (N_CORE, ny, run, quarter))
    vmem("core_in", (ny, run, quarter))
    names.add("core_ssem", pltpu.SemaphoreType.DMA)
    names.add("core_rsem", pltpu.SemaphoreType.DMA)
    vmem("sum_y", (1, ny, run, quarter))
    vmem("in_y", (1, ny, run, quarter))
    sems("ex_y", 1, ny)
    vmem("sum_z", (1, nz, N_MP * per, quarter))
    vmem("in_z", (1, nz, N_MP * per, quarter))
    sems("ex_z", 1, nz)
    vmem("last_a", (1, N_MP, per, quarter), F32)
    vmem("last_b", (1, N_MP, per, quarter), F32)
    sems("last", 1, N_MP)
    return names


def local(nz, nyc, attn, out_proj, tangent_proj, resid, target, routes, gates, w_gate, w_up, w_down):
    tokens, quarter = attn.shape
    hidden = w_gate.shape[2]
    experts = nz * nyc
    cap = max(2, 5 * 2 * tokens // (4 * experts))
    half = nyc * cap
    rows = nz * 2 * half
    sizes = (nz, nyc, cap, tokens, quarter, hidden, CHUNKS, BACK_CHUNKS)

    flat = routes.reshape(-1)
    number = jnp.arange(flat.shape[0])
    earlier = (flat[:, None] == flat[None, :]) & (number[None, :] < number[:, None])
    slot = flat * cap + jnp.sum(earlier.astype(jnp.int32), axis=1)
    place = (slot // half) * (2 * half) + slot % half
    place = place.reshape(tokens, 2)
    place = jnp.stack([place, place + half], 0).reshape(2 * tokens, 2)
    line = jnp.arange(rows)
    back0 = (place[:, 0:1] == line[None, :]).astype(BF)
    back1 = (place[:, 1:2] == line[None, :]).astype(BF)
    pick = ((line[:, None] == place[None, :, 0]) | (line[:, None] == place[None, :, 1])).astype(BF)
    gates2 = jnp.concatenate([gates, gates], 0)
    slot_gate = jnp.sum(
        jnp.where(line[:, None] == place[None, :, 0], gates2[None, :, 0], 0.0)
        + jnp.where(line[:, None] == place[None, :, 1], gates2[None, :, 1], 0.0),
        axis=1,
        keepdims=True,
    )
    names = scratch(sizes)
    vmem, anywhere = pl.BlockSpec(memory_space=pltpu.VMEM), pl.BlockSpec(memory_space=pl.ANY)
    return pl.pallas_call(
        functools.partial(kernel, sizes, names),
        out_shape=jax.ShapeDtypeStruct((1, quarter // experts, N_MP * quarter), F32),
        in_specs=[anywhere] * 3 + [vmem] * 7 + [anywhere] * 3,
        out_specs=vmem,
        scratch_shapes=names.shapes,
        compiler_params=pltpu.CompilerParams(
            collective_id=0, has_side_effects=True, vmem_limit_bytes=60 * 2**20
        ),
        cost_estimate=pl.CostEstimate(flops=6_000_000_000, bytes_accessed=12_000_000, transcendentals=300_000),
    )(
        attn, out_proj, tangent_proj, resid, target, pick, back0, back1, slot_gate, gates2, w_gate, w_up, w_down
    )


def solution(mesh):
    experts = mesh.shape["expert"]
    nz = 1 << ((experts.bit_length() - 1) // 2)
    in_specs = (
        P("expert", "mp"),
        P("mp", None),
        P("mp", None),
        P("expert", "mp"),
        P("expert", "mp"),
        P("expert", None),
        P("expert", None),
        P("expert", None, "mp"),
        P("expert", None, "mp"),
        P("expert", "mp", None),
    )
    return jax.shard_map(
        functools.partial(local, nz, experts // nz),
        mesh=mesh,
        in_specs=in_specs,
        out_specs=P("mp", "expert", None),
        check_vma=False,
    )
```

```python
import functools
import math

import jax
import jax.numpy as jnp
from jax import lax
from jax.experimental import pallas as pl
from jax.experimental.pallas import tpu as pltpu
from jax.sharding import PartitionSpec as P

MESH = pl.DeviceIdType.MESH
BF = jnp.bfloat16
F32 = jnp.float32
N_MP = 4
N_CORE = 2
CHUNKS = 4
BACK_CHUNKS = 2
ORDER_IN = (2, 3, 2, 1, 0, 2, 0, 1, 1, 2, 3, 1, 0, 3, 2, 3, 0, 1, 2, 1, 3, 2, 0, 1, 3, 0, 3, 1, 2, 0, 3, 0)
ORDER_OUT = (0, 3, 0, 0, 3, 3, 0, 2, 2, 3, 1, 0, 2, 3, 1, 1, 2, 0, 3, 1, 2, 1, 0, 3, 2, 3, 0, 1, 2, 3, 0, 1, 2, 1, 2, 1, 3, 0, 2, 1)
ORDER_BACK = (0, 0, 1, 0, 1, 1, 0, 1, 0, 1, 0, 1, 0, 0, 1, 1, 0, 1)


class Names:
    def __init__(self):
        self.names, self.shapes = [], []

    def add(self, name, shape):
        self.names.append(name)
        self.shapes.append(shape)

    def bind(self, refs):
        for name, ref in zip(self.names, refs, strict=True):
            setattr(self, name, ref)


def dot(left, right):
    return jnp.dot(left, right, preferred_element_type=F32)


def dot_last(left, right):
    return lax.dot_general(left, right, (((1,), (1,)), ((), ())), preferred_element_type=F32)


def dot_first(left, right):
    return lax.dot_general(left, right, (((0,), (0,)), ((), ())), preferred_element_type=F32)


def silu_terms(gate_pre):
    sigma = jax.nn.sigmoid(gate_pre)
    silu_val = gate_pre * sigma
    silu_one = sigma * (1.0 + gate_pre * (1.0 - sigma))
    silu_two = sigma * (1.0 - sigma) * (2.0 + gate_pre * (1.0 - 2.0 * sigma))
    return (silu_val, silu_one, silu_two)


def each(lower, upper, body):
    def step(i, carry):
        body(i)
        return carry

    lax.fori_loop(lower, upper, step, 0)


def pipeline(stages, order):
    done = [0] * (max(order) + 1)
    for k in order:
        stages[done[k]](k)
        done[k] += 1


class Exchange:
    def __init__(self, src, dst, sems, n, me, device):
        self.src, self.dst, self.n, self.me, self.device = src, dst, n, me, device
        self.ssem, self.rsem = sems

    def copy(self, k, d, block, landing, device):
        return pltpu.make_async_remote_copy(
            src_ref=self.src.at[k, block],
            dst_ref=self.dst.at[k, landing],
            send_sem=self.ssem.at[k, d],
            recv_sem=self.rsem.at[k, d],
            device_id=device,
            device_id_type=MESH,
        )

    def out(self, k, d):
        to = lax.rem(self.me + d, self.n)
        return self.copy(k, d, to, self.me, self.device(to))

    def start(self, k):
        each(1, self.n, lambda d: self.out(k, d).start())
        self.dst[k, pl.ds(self.me, 1)] = self.src[k, pl.ds(self.me, 1)]

    def wait(self, k):
        def body(d):
            source = lax.rem(self.me + self.n - d, self.n)
            self.copy(k, d, source, source, self.device(source)).wait_recv()

        each(1, self.n, body)

    def drain(self, k):
        each(1, self.n, lambda d: self.out(k, d).wait_send())


class SpreadY(Exchange):
    def __init__(self, ref, core, sems, n, me, device):
        super().__init__(ref, ref, sems, n, me, device)
        self.core = core

    def copy(self, k, d, block, landing, device):
        ref = self.src.at[k, self.core, block]
        return pltpu.make_async_remote_copy(
            src_ref=ref,
            dst_ref=ref,
            send_sem=self.ssem.at[k, d],
            recv_sem=self.rsem.at[k, d],
            device_id=device,
            device_id_type=MESH,
        )

    def out(self, k, d):
        to = lax.rem(self.me + d, self.n)
        return self.copy(k, d, self.me, self.me, self.device(to))

    def start(self, k):
        each(1, self.n, lambda d: self.out(k, d).start())


class Ring:
    def __init__(self):
        self.expert = lax.axis_index("expert")
        self.me = lax.axis_index("mp")
        self.right = lax.rem(self.me + 1, N_MP)
        self.left = lax.rem(self.me + N_MP - 1, N_MP)
        self.opp = lax.rem(self.me + 2, N_MP)

    def copy(self, src, dst, ssem, rsem, to):
        return pltpu.make_async_remote_copy(
            src_ref=src,
            dst_ref=dst,
            send_sem=ssem,
            recv_sem=rsem,
            device_id=(self.expert, to),
            device_id_type=MESH,
        )


class Scatter:
    def __init__(self, ring, part, hop, total, sems, rows):
        self.ring, self.part, self.hop, self.total, self.rows = ring, part, hop, total, rows
        self.ssem, self.rsem = sems
        self.half = rows // 2

    def copy(self, k, i):
        r, h = self.ring, self.half
        first, second = pl.ds(0, h), pl.ds(h, h)
        part, hop, total = self.part.at[k], self.hop.at[k], self.total.at[k]
        plan = (
            (part.at[r.opp, first], hop.at[0], r.left),
            (part.at[r.opp, second], hop.at[1], r.right),
            (part.at[r.left, second], total.at[0, second], r.left),
            (part.at[r.right, first], total.at[1, first], r.right),
            (part.at[r.left, first], total.at[0, first], r.left),
            (part.at[r.right, second], total.at[1, second], r.right),
        )
        src, dst, to = plan[i]
        return r.copy(src, dst, self.ssem.at[k, i], self.rsem.at[k, i], to)

    def start(self, k, index):
        self.copy(k, index).start()

    def middle(self, k):
        r, h = self.ring, self.half
        self.copy(k, 0).wait_recv()
        self.add(k, r.left, pl.ds(0, h), 0)
        self.copy(k, 4).start()
        self.copy(k, 1).wait_recv()
        self.add(k, r.right, pl.ds(h, h), 1)
        self.copy(k, 5).start()

    def add(self, k, block, rows, side):
        value = self.part[k, pl.ds(block, 1), rows, :][0].astype(F32) + self.hop[k, side].astype(F32)
        self.part[k, pl.ds(block, 1), rows, :] = value.astype(BF)[None]

    def finish(self, k):
        for i in (2, 3, 4, 5):
            self.copy(k, i).wait_recv()
        own = self.part[k, pl.ds(self.ring.me, 1)][0].astype(F32)
        return own + self.total[k, 0].astype(F32) + self.total[k, 1].astype(F32)

    def drain(self, k):
        for i in range(6):
            self.copy(k, i).wait_send()


class Gather:
    def __init__(self, ring, full, sems, rows):
        self.ring, self.full = ring, full
        self.ssem, self.rsem = sems
        self.half = rows // 2

    def move(self, k, i, block, rows, to):
        ref = self.full.at[k, block, rows]
        return self.ring.copy(ref, ref, self.ssem.at[k, i], self.rsem.at[k, i], to)

    def copy(self, k, i):
        r, h = self.ring, self.half
        first, second = pl.ds(0, h), pl.ds(h, h)
        plan = (
            (r.me, first, r.left),
            (r.me, second, r.right),
            (r.me, second, r.left),
            (r.me, first, r.right),
            (r.right, first, r.left),
            (r.left, second, r.right),
        )
        return self.move(k, i, *plan[i])

    def arrival(self, k, i):
        r, h = self.ring, self.half
        first, second = pl.ds(0, h), pl.ds(h, h)
        plan = (
            (r.right, first),
            (r.left, second),
            (r.right, second),
            (r.left, first),
            (r.opp, first),
            (r.opp, second),
        )
        return self.move(k, i, *plan[i], r.left)

    def start(self, k):
        for i in range(4):
            self.copy(k, i).start()

    def middle(self, k):
        for i in range(2):
            self.arrival(k, i).wait_recv()
            self.copy(k, 4 + i).start()

    def finish(self, k):
        for i in range(2, 6):
            self.arrival(k, i).wait_recv()

    def drain(self, k):
        for i in range(6):
            self.copy(k, i).wait_send()


def iota(shape, dim):
    return lax.broadcasted_iota(jnp.int32, shape, dim)


def kernel(sizes, names, *refs):
    attn_h, out_proj_h, tan_proj_h, resid, target, routes, gates, w_gate_h, w_up_h, w_down_h, out = refs[:11]
    s = names
    s.bind(refs[11:])
    nz, nyc, cap, tokens, quarter, hidden, chunks, back_chunks = sizes
    ny = nyc // N_CORE
    cw = quarter // chunks
    bw = quarter // 2 // back_chunks
    half = nz * cap
    block = 2 * half
    rows = nyc * block
    model = N_MP * quarter

    ring = Ring()
    me_e, me_m = ring.expert, ring.me
    z, yc = lax.div(me_e, nyc), lax.rem(me_e, nyc)
    y, core = lax.div(yc, N_CORE), lax.rem(yc, N_CORE)

    def at_z(to):
        return (to * nyc + yc, me_m)

    def at_yc(to):
        return (z * nyc + to, me_m)

    loads = [
        pltpu.make_async_copy(src, dst, s.load_sem.at[i])
        for i, (src, dst) in enumerate(
            (
                (attn_h, s.attn),
                (out_proj_h, s.out_proj),
                (tan_proj_h, s.tan_proj),
                (w_gate_h.at[0], s.w_gate),
                (w_up_h.at[0], s.w_up),
                (w_down_h.at[0], s.w_down),
            )
        )
    ]
    for load in loads:
        load.start()

    barrier = pltpu.get_barrier_semaphore()
    counts = {}

    def nth(stage):
        counts[stage] = counts.get(stage, -1) + 1
        return counts[stage]

    def greet(device):
        pl.semaphore_signal(barrier, inc=1, device_id=device, device_id_type=MESH)

    each(1, nz, lambda d: greet(at_z(lax.rem(z + d, nz))))
    each(1, nyc, lambda d: greet(at_yc(lax.rem(yc + d, nyc))))
    each(1, N_MP, lambda d: greet((me_e, lax.rem(me_m + d, N_MP))))

    def sems(name):
        return getattr(s, name + "_ssem"), getattr(s, name + "_rsem")

    scat_z = Scatter(ring, s.part_z, s.hop_z, s.total_z, sems("scat_z"), 2 * tokens)
    go_z = Exchange(s.go_a, s.go_b, sems("go_z"), nz, z, at_z)
    go_yc = Exchange(s.go_c, s.go_d, sems("go_yc"), nyc, yc, at_yc)
    gather_x = Gather(ring, s.x_full, sems("gather_x"), rows)
    scat_o = Scatter(ring, s.part_o, s.hop_o, s.total_o, sems("scat_o"), rows)
    ret_yc = Exchange(s.ret_a, s.ret_b, sems("ret_yc"), nyc, yc, at_yc)
    ret_z = Exchange(s.ret_c, s.ret_d, sems("ret_z"), nz, z, at_z)
    cot_z = Exchange(s.cot_a, s.cot_b, sems("cot_z"), nz, z, at_z)
    cot_yc = Exchange(s.cot_c, s.cot_d, sems("cot_yc"), nyc, yc, at_yc)
    gather_c = Gather(ring, s.c_full, sems("gather_c"), rows)
    scat_b = Scatter(ring, s.part_b, s.hop_b, s.total_b, sems("scat_b"), rows)
    bak_yc = Exchange(s.bak_a, s.bak_b, sems("bak_yc"), nyc, yc, at_yc)
    bak_z = Exchange(s.bak_c, s.bak_d, sems("bak_z"), nz, z, at_z)
    att_yc = Exchange(s.att_a, s.att_b, sems("att_yc"), nyc, yc, at_yc)
    gather_a = Gather(ring, s.att_full, sems("gather_a"), quarter)
    spread_y = SpreadY(s.dx, core, sems("spread_y"), ny, y, lambda to: at_yc(to * N_CORE + core))
    ex_z = Exchange(s.sum_z, s.in_z, sems("ex_z"), nz, z, at_z)
    last = Exchange(s.last_a, s.last_b, sems("last"), N_MP, me_m, lambda to: (me_e, to))

    def swap(src, dst, k, width):
        value = dot(s.swap[...], src[k].reshape(rows, width))
        dst[k] = value.astype(BF).reshape(nyc, block, width)

    loads[0].wait()
    loads[1].wait()
    loads[2].wait()

    def z_part(k, q):
        columns = pl.ds(pl.multiple_of(q * quarter + k * cw, 128), cw)
        s.part_z[k, pl.ds(q, 1), pl.ds(0, tokens), :] = dot(s.attn[...], s.out_proj[:, columns]).astype(BF)[None]
        s.part_z[k, pl.ds(q, 1), pl.ds(tokens, tokens), :] = dot(s.attn[...], s.tan_proj[:, columns]).astype(BF)[None]

    def z_first(k):
        z_part(k, ring.opp)
        if nth("z_first") == 0:
            pl.semaphore_wait(barrier, nz + nyc + N_MP - 3)
        scat_z.start(k, 0)
        scat_z.start(k, 1)

    def z_second(k):
        z_part(k, ring.left)
        scat_z.start(k, 2)
        z_part(k, ring.right)
        scat_z.start(k, 3)
        z_part(k, ring.me)
        if nth("z_second") == 0:
            route_rows()

    def route_rows():
        eye = iota((tokens, tokens), 0) == iota((tokens, tokens), 1)
        earlier_row = (iota((tokens, tokens), 1) < iota((tokens, tokens), 0)).astype(F32)
        earlier_column = (iota((tokens, tokens), 0) < iota((tokens, tokens), 1)).astype(F32)

        def column(row, zero):
            return jnp.sum(jnp.where(eye, row, zero), axis=1, keepdims=True)

        first, second = routes[0:1, :], routes[1:2, :]
        gate_rows = gates[0:1, :], gates[1:2, :]
        names_f = [first.astype(F32), second.astype(F32)]
        columns_f = [column(row, 0.0) for row in names_f]
        same = [[(columns_f[i] == names_f[j]).astype(F32) for j in range(2)] for i in range(2)]

        def line_of(name, position):
            wide, narrow = lax.div(name, nyc), lax.rem(name, nyc)
            return wide * block + narrow * cap + position

        place_row = [
            line_of(first, jnp.sum(same[0][0] * earlier_column, axis=0, keepdims=True).astype(jnp.int32)),
            line_of(
                second,
                (
                    jnp.sum(same[0][1], axis=0, keepdims=True)
                    + jnp.sum(same[1][1] * earlier_column, axis=0, keepdims=True)
                ).astype(jnp.int32),
            ),
        ]
        place_column = [
            line_of(
                columns_f[0].astype(jnp.int32),
                jnp.sum(same[0][0] * earlier_row, axis=1, keepdims=True).astype(jnp.int32),
            ),
            line_of(
                columns_f[1].astype(jnp.int32),
                (
                    jnp.sum(same[1][0], axis=1, keepdims=True)
                    + jnp.sum(same[1][1] * earlier_row, axis=1, keepdims=True)
                ).astype(jnp.int32),
            ),
        ]
        across, down = iota((tokens, rows), 1), iota((rows, tokens), 0)
        weight = jnp.zeros((rows, 1), F32)
        for h in range(2):
            at = pl.ds(h * tokens, tokens)
            s.back0[at, :] = (across == place_column[0] + h * half).astype(F32).astype(BF)
            s.back1[at, :] = (across == place_column[1] + h * half).astype(F32).astype(BF)
            hits = [down == place_row[i] + h * half for i in range(2)]
            s.pick[:, at] = (hits[0] | hits[1]).astype(F32).astype(BF)
            chosen = jnp.where(hits[0], gate_rows[0], 0.0) + jnp.where(hits[1], gate_rows[1], 0.0)
            weight = weight + jnp.sum(chosen, axis=1, keepdims=True)
        s.slot_gate[...] = weight
        both = [column(row, 0.0) for row in gate_rows]
        for i in range(2):
            s.gate_column[i] = jnp.concatenate([both[i], both[i]], 0)

    def swap_rows():
        r = iota((rows, 1), 0)
        a, h, b, p = r // block, (r % block) // half, (r % half) // cap, r % cap
        s.swap[...] = (iota((rows, rows), 1) == b * block + h * half + a * cap + p).astype(F32).astype(BF)

    def spread_x(k):
        value = scat_z.finish(k)
        columns = pl.ds(k * cw, cw)
        s.x_in[k, pl.ds(0, tokens), :] = (
            resid[:, columns].astype(F32) + value[:tokens]
        ).astype(BF)
        s.x_in[k, pl.ds(tokens, tokens), :] = value[tokens:].astype(BF)
        s.go_a[k] = dot(s.pick[...], s.x_in[k]).astype(BF).reshape(nz, block, cw)
        go_z.start(k)
        before = nth("spread_x")
        if before == 0:
            swap_rows()
        if before == chunks - 1:
            attn_send()

    def pass_x(k):
        go_z.wait(k)
        swap(s.go_b, s.go_c, k, cw)
        go_yc.start(k)

    def gather_start_x(k):
        go_yc.wait(k)
        s.x_full[k, pl.ds(me_m, 1)] = s.go_d[k].reshape(1, rows, cw)
        gather_x.start(k)

    step_rows = 2 * block

    def pre_acts(k):
        gather_x.finish(k)
        before = nth("pre_acts")
        if before == 0:
            loads[3].wait()
            loads[4].wait()

        def body(i):
            at = pl.ds(pl.multiple_of(i * step_rows, step_rows), step_rows)
            gate = jnp.zeros((step_rows, hidden), F32)
            up = jnp.zeros((step_rows, hidden), F32)
            for m in range(N_MP):
                features = pl.ds(m * quarter + k * cw, cw)
                values = s.x_full[k, m, at, :]
                gate = gate + dot_last(values, s.w_gate[:, features])
                up = up + dot_last(values, s.w_up[:, features])
            if before:
                gate = gate + s.gate[at, :]
                up = up + s.up[at, :]
            s.gate[at, :] = gate
            s.up[at, :] = up

        each(0, rows // step_rows, body)

    per = quarter // (nz * nyc)
    run = nz * per

    def attn_send():
        r = iota((quarter, 1), 0)
        c, zz, p = r // run, (r % run) // per, r % per
        wanted = (zz * nyc + c) * per + p
        permute = (iota((quarter, quarter), 1) == wanted).astype(F32).astype(BF)
        s.att_a[0] = dot_last(permute, s.attn[...]).astype(BF).reshape(nyc, run, tokens)
        att_yc.start(0)

    def attn_gather():
        att_yc.wait(0)
        s.att_full[0, pl.ds(me_m, 1)] = s.att_b[0].reshape(1, nyc * run, tokens)
        gather_a.start(0)

    pipeline((z_first, z_second, scat_z.middle, spread_x, pass_x, gather_start_x, gather_x.middle, pre_acts), ORDER_IN)
    attn_gather()

    def activations(i):
        at, tan_at = pl.ds(pl.multiple_of(i * block, 8), half), pl.ds(pl.multiple_of(i * block + half, 8), half)
        gate_pre, gate_tan = s.gate[at, :], s.gate[tan_at, :]
        up_pre, up_tan = s.up[at, :], s.up[tan_at, :]
        silu_val, silu_one, _ = silu_terms(gate_pre)
        hid = silu_val * up_pre
        hid_tan = silu_one * gate_tan * up_pre + silu_val * up_tan
        s.hidden[pl.ds(pl.multiple_of(i * block, 16), block), :] = jnp.concatenate([hid, hid_tan], 0).astype(BF)

    each(0, nyc, activations)
    loads[5].wait()

    def o_part(k, q):
        columns = pl.ds(pl.multiple_of(q * quarter + k * cw, 128), cw)
        s.part_o[k, pl.ds(q, 1)] = dot(s.hidden[...], s.w_down[:, columns]).astype(BF)[None]

    def o_first(k):
        o_part(k, ring.opp)
        scat_o.start(k, 0)
        scat_o.start(k, 1)

    def o_second(k):
        o_part(k, ring.left)
        scat_o.start(k, 2)
        o_part(k, ring.right)
        scat_o.start(k, 3)
        o_part(k, ring.me)

    def return_o(k):
        s.ret_a[k] = scat_o.finish(k).astype(BF).reshape(nyc, block, cw)
        ret_yc.start(k)

    def pass_o(k):
        ret_yc.wait(k)
        swap(s.ret_b, s.ret_c, k, cw)
        ret_z.start(k)

    def combine(values):
        return s.gate_column[0] * dot(s.back0[...], values) + s.gate_column[1] * dot(s.back1[...], values)

    def residual(k):
        ret_z.wait(k)
        columns = pl.ds(k * cw, cw)
        both = s.x_in[k].astype(F32) + combine(s.ret_d[k].reshape(rows, cw))
        s.y_tan[:, columns] = both[tokens:]
        diff = both[:tokens] - target[:, columns].astype(F32)
        sent = jnp.concatenate([diff, both[tokens:]], 0).astype(BF)
        s.cot_a[k] = (dot(s.pick[...], sent) * s.slot_gate[...]).astype(BF).reshape(nz, block, cw)
        cot_z.start(k)

    def pass_c(k):
        cot_z.wait(k)
        swap(s.cot_b, s.cot_c, k, cw)
        cot_yc.start(k)

    def gather_start_c(k):
        cot_yc.wait(k)
        s.c_full[k, pl.ds(me_m, 1)] = s.cot_d[k].reshape(1, rows, cw)
        gather_c.start(k)

    def grad_hidden(k):
        gather_c.finish(k)
        before = nth("grad_hidden")

        def body(i):
            at = pl.ds(pl.multiple_of(i * step_rows, step_rows), step_rows)
            grad = jnp.zeros((step_rows, hidden), F32)
            for m in range(N_MP):
                features = pl.ds(m * quarter + k * cw, cw)
                grad = grad + dot_last(s.c_full[k, m, at, :], s.w_down[:, features])
            if before:
                grad = grad + s.grad[at, :]
            s.grad[at, :] = grad

        each(0, rows // step_rows, body)

    pipeline(
        (
            o_first,
            o_second,
            scat_o.middle,
            return_o,
            pass_o,
            residual,
            pass_c,
            gather_start_c,
            gather_c.middle,
            grad_hidden,
        ),
        ORDER_OUT,
    )
    gather_a.middle(0)

    def tangents(i):
        at, tan_at = pl.ds(pl.multiple_of(i * block, 8), half), pl.ds(pl.multiple_of(i * block + half, 8), half)
        gate_pre, gate_tan = s.gate[at, :], s.gate[tan_at, :]
        up_pre, up_tan = s.up[at, :], s.up[tan_at, :]
        dh, dh_tan = s.grad[at, :], s.grad[tan_at, :]
        silu_val, silu_one, silu_two = silu_terms(gate_pre)
        da_tan = (dh_tan * up_pre + dh * up_tan) * silu_one + dh * up_pre * silu_two * gate_tan
        db_tan = dh_tan * silu_val + dh * silu_one * gate_tan
        to = pl.ds(pl.multiple_of(i * half, 8), half)
        s.da_tan[to, :] = da_tan
        s.db_tan[to, :] = db_tan

    each(0, nyc, tangents)

    def b_part(k, q):
        da_tan, db_tan = s.da_tan[...].astype(BF), s.db_tan[...].astype(BF)
        sides = []
        for h in range(2):
            features = pl.ds(pl.multiple_of(q * quarter + h * (quarter // 2) + k * bw, 128), bw)
            term = dot(da_tan, s.w_gate[:, features]) + dot(db_tan, s.w_up[:, features])
            sides.append(term.reshape(nyc, half, bw))
        s.part_b[k, pl.ds(q, 1)] = jnp.concatenate(sides, 1).astype(BF).reshape(1, rows, bw)

    def b_first(k):
        b_part(k, ring.opp)
        scat_b.start(k, 0)
        scat_b.start(k, 1)

    def b_second(k):
        b_part(k, ring.left)
        scat_b.start(k, 2)
        b_part(k, ring.right)
        scat_b.start(k, 3)
        b_part(k, ring.me)

    def return_b(k):
        s.bak_a[k] = scat_b.finish(k).astype(BF).reshape(nyc, block, bw)
        bak_yc.start(k)

    def pass_b(k):
        bak_yc.wait(k)
        swap(s.bak_b, s.bak_c, k, bw)
        bak_z.start(k)

    def grad_in(k):
        bak_z.wait(k)
        both = combine(s.bak_d[k].reshape(rows, bw))
        for h in range(2):
            columns = pl.ds(h * (quarter // 2) + k * bw, bw)
            value = (s.y_tan[:, columns] + both[h * tokens : (h + 1) * tokens]).astype(BF)
            s.dx[k, pl.ds(core, 1), pl.ds(y, 1), :, pl.ds(h * bw, bw)] = value.reshape(1, 1, tokens, bw)
        spread_y.start(k)

    other = 1 - core

    def core_copy(k, side):
        return pltpu.make_async_remote_copy(
            src_ref=s.dx.at[k, side],
            dst_ref=s.dx.at[k, side],
            send_sem=s.core_ssem.at[k],
            recv_sem=s.core_rsem.at[k],
            device_id=at_yc(y * N_CORE + other),
            device_id_type=MESH,
        )

    def dx_core(k):
        spread_y.wait(k)
        core_copy(k, core).start()

    def attn_rows():
        gather_a.finish(0)
        for c in range(N_CORE):
            for yy in range(ny):
                columns = pl.ds((c * ny + yy) * tokens, tokens)
                for m in range(N_MP):
                    source = pl.ds((yy * N_CORE + c) * run, run)
                    s.att_rows[pl.ds(m * run, run), columns] = s.att_full[0, m, source, :]

    def product(k):
        if nth("product") == 0:
            attn_rows()
        core_copy(k, other).wait_recv()
        value = dot(s.att_rows[...], s.dx[k].reshape(nyc * tokens, 2 * bw))
        value = value.reshape(N_MP, nz, per, 2 * bw)
        value = jnp.stack([value[m] for m in range(N_MP)], 1)
        s.sum_z[k] = value.reshape(nz, N_MP * per, 2 * bw).astype(BF)
        ex_z.start(k)

    def total_z(k):
        ex_z.wait(k)
        total = jnp.sum(s.in_z[k].astype(F32), axis=0) * (1.0 / math.sqrt(tokens * nz * nyc))
        total = total.reshape(N_MP, per, 2 * bw)
        for h in range(2):
            columns = pl.ds(h * (quarter // 2) + k * bw, bw)
            s.last_a[0, :, :, columns] = total[:, :, h * bw : (h + 1) * bw]

    pipeline(
        (b_first, b_second, scat_b.middle, return_b, pass_b, grad_in, dx_core, product, total_z),
        ORDER_BACK,
    )
    last.start(0)
    last.wait(0)
    for m in range(N_MP):
        out[0, :, m * quarter : (m + 1) * quarter] = s.last_b[0, m]

    for k in range(chunks):
        for stage in (scat_z, go_z, go_yc, gather_x, scat_o, ret_yc, ret_z, cot_z, cot_yc, gather_c):
            stage.drain(k)
    for k in range(back_chunks):
        for stage in (scat_b, bak_yc, bak_z, spread_y, ex_z):
            stage.drain(k)
        core_copy(k, core).wait_send()
    att_yc.drain(0)
    gather_a.drain(0)
    last.drain(0)


def scratch(sizes):
    nz, nyc, cap, tokens, quarter, hidden, chunks, back_chunks = sizes
    ny = nyc // N_CORE
    cw, bw = quarter // chunks, quarter // 2 // back_chunks
    block = 2 * nz * cap
    rows = nyc * block
    model = N_MP * quarter
    per = quarter // (nz * nyc)
    names = Names()

    def vmem(name, shape, kind=BF):
        names.add(name, pltpu.VMEM(shape, kind))

    def sems(name, k, n):
        names.add(name + "_ssem", pltpu.SemaphoreType.DMA((k, n)))
        names.add(name + "_rsem", pltpu.SemaphoreType.DMA((k, n)))

    names.add("load_sem", pltpu.SemaphoreType.DMA((6,)))
    vmem("attn", (tokens, quarter))
    vmem("out_proj", (quarter, model))
    vmem("tan_proj", (quarter, model))
    vmem("w_gate", (hidden, model))
    vmem("w_up", (hidden, model))
    vmem("w_down", (hidden, model))
    vmem("swap", (rows, rows))
    for tag, count, height, width in (
        ("z", chunks, 2 * tokens, cw),
        ("o", chunks, rows, cw),
        ("b", back_chunks, rows, bw),
    ):
        vmem("part_" + tag, (count, N_MP, height, width))
        vmem("hop_" + tag, (count, 2, height // 2, width))
        vmem("total_" + tag, (count, 2, height, width))
        sems("scat_" + tag, count, 6)
    for tag, count, width in (("go", chunks, cw), ("ret", chunks, cw), ("cot", chunks, cw), ("bak", back_chunks, bw)):
        for letter in "abcd":
            vmem(f"{tag}_{letter}", (count, nz, block, width))
        sems(tag + "_z", count, nz)
        sems(tag + "_yc", count, nyc)
    for tag in "xc":
        vmem(tag + "_full", (chunks, N_MP, rows, cw))
        sems("gather_" + tag, chunks, 6)
    run = nz * per
    for letter in "ab":
        vmem("att_" + letter, (1, nyc, run, tokens))
    sems("att_yc", 1, nyc)
    vmem("att_full", (1, N_MP, nyc * run, tokens))
    sems("gather_a", 1, 6)
    vmem("att_rows", (N_MP * run, nyc * tokens))
    vmem("pick", (rows, 2 * tokens))
    vmem("back0", (2 * tokens, rows))
    vmem("back1", (2 * tokens, rows))
    vmem("slot_gate", (rows, 1), F32)
    vmem("gate_column", (2, 2 * tokens, 1), F32)
    vmem("x_in", (chunks, 2 * tokens, cw))
    vmem("gate", (rows, hidden), F32)
    vmem("up", (rows, hidden), F32)
    vmem("grad", (rows, hidden), F32)
    vmem("hidden", (rows, hidden))
    vmem("da_tan", (rows // 2, hidden), F32)
    vmem("db_tan", (rows // 2, hidden), F32)
    vmem("y_tan", (tokens, quarter), F32)
    vmem("dx", (back_chunks, N_CORE, ny, tokens, 2 * bw))
    sems("spread_y", back_chunks, ny)
    names.add("core_ssem", pltpu.SemaphoreType.DMA((back_chunks,)))
    names.add("core_rsem", pltpu.SemaphoreType.DMA((back_chunks,)))
    vmem("sum_z", (back_chunks, nz, N_MP * per, 2 * bw))
    vmem("in_z", (back_chunks, nz, N_MP * per, 2 * bw))
    sems("ex_z", back_chunks, nz)
    vmem("last_a", (1, N_MP, per, quarter), F32)
    vmem("last_b", (1, N_MP, per, quarter), F32)
    sems("last", 1, N_MP)
    return names


def local(nz, nyc, attn, out_proj, tangent_proj, resid, target, routes, gates, w_gate, w_up, w_down):
    tokens, quarter = attn.shape
    hidden = w_gate.shape[2]
    experts = nz * nyc
    cap = max(2, 5 * 2 * tokens // (4 * experts))
    sizes = (nz, nyc, cap, tokens, quarter, hidden, CHUNKS, BACK_CHUNKS)
    names = scratch(sizes)
    vmem, anywhere = pl.BlockSpec(memory_space=pltpu.VMEM), pl.BlockSpec(memory_space=pl.ANY)
    return pl.pallas_call(
        functools.partial(kernel, sizes, names),
        out_shape=jax.ShapeDtypeStruct((1, quarter // experts, N_MP * quarter), F32),
        in_specs=[anywhere] * 3 + [vmem] * 4 + [anywhere] * 3,
        out_specs=vmem,
        scratch_shapes=names.shapes,
        compiler_params=pltpu.CompilerParams(
            collective_id=0, has_side_effects=True, vmem_limit_bytes=60 * 2**20
        ),
        cost_estimate=pl.CostEstimate(flops=6_000_000_000, bytes_accessed=12_000_000, transcendentals=300_000),
    )(
        attn,
        out_proj,
        tangent_proj,
        resid,
        target,
        routes.T,
        gates.T,
        jnp.swapaxes(w_gate, 1, 2),
        jnp.swapaxes(w_up, 1, 2),
        w_down,
    )


def solution(mesh):
    experts = mesh.shape["expert"]
    nz = 1 << ((experts.bit_length() - 1) // 2)
    in_specs = (
        P("expert", "mp"),
        P("mp", None),
        P("mp", None),
        P("expert", "mp"),
        P("expert", "mp"),
        P("expert", None),
        P("expert", None),
        P("expert", None, "mp"),
        P("expert", None, "mp"),
        P("expert", "mp", None),
    )
    return jax.shard_map(
        functools.partial(local, nz, experts // nz),
        mesh=mesh,
        in_specs=in_specs,
        out_specs=P("mp", "expert", None),
        check_vma=False,
    )
```

```python
import functools
import math

import jax
import jax.numpy as jnp
from jax import lax
from jax.experimental import pallas as pl
from jax.experimental.pallas import tpu as pltpu
from jax.sharding import PartitionSpec as P

MESH = pl.DeviceIdType.MESH
BF = jnp.bfloat16
F32 = jnp.float32
N_MP = 4
N_CORE = 2
CHUNKS = 4
BACK_CHUNKS = 2
PARTS = 2
ORDER = (
    ("z1", 3, 0), ("z1", 1, 0), ("z2", 3, 0), ("z1", 2, 0), ("zm", 3, 0), ("z2", 1, 0), ("z1", 0, 0),
    ("zm", 1, 0), ("sp", 3, 0), ("z2", 2, 0), ("zm", 2, 0), ("z2", 0, 0), ("sp", 1, 0), ("zm", 0, 0),
    ("sp", 0, 0), ("pa", 3, 0), ("sp", 2, 0), ("pa", 1, 0), ("gs", 3, 0), ("gs", 3, 1), ("pa", 0, 0),
    ("gs", 1, 0), ("gm", 3, 0), ("gs", 1, 1), ("pa", 2, 0), ("gs", 0, 0), ("gm", 1, 0), ("pr", 3, 0),
    ("gs", 2, 0), ("gm", 0, 0), ("gs", 2, 1), ("gm", 2, 0), ("gs", 0, 1), ("gm", 3, 1), ("pr", 0, 0),
    ("pr", 1, 0), ("gm", 1, 1), ("gm", 2, 1), ("pr", 2, 0), ("ac", 0, 0), ("gm", 0, 1), ("o1", 2, 0),
    ("o1", 1, 0), ("o1", 3, 0), ("o2", 1, 0), ("pr", 3, 1), ("pr", 1, 1), ("pr", 2, 1), ("pr", 0, 1),
    ("ac", 0, 1), ("o1", 1, 1), ("om", 1, 0), ("o1", 2, 1), ("o2", 1, 1), ("om", 1, 1), ("o2", 2, 1),
    ("o2", 2, 0), ("om", 2, 0), ("o2", 3, 0), ("om", 2, 1), ("om", 3, 0), ("o1", 0, 0), ("o1", 3, 1),
    ("rt", 1, 0), ("o1", 0, 1), ("rt", 2, 0), ("po", 1, 0), ("o2", 0, 1), ("o2", 3, 1), ("om", 3, 1),
    ("po", 2, 0), ("o2", 0, 0), ("om", 0, 0), ("rt", 3, 0), ("re", 1, 0), ("om", 0, 1), ("po", 3, 0),
    ("re", 2, 0), ("rt", 0, 0), ("pc", 1, 0), ("po", 0, 0), ("re", 3, 0), ("cs", 1, 0), ("cs", 1, 1),
    ("pc", 2, 0), ("re", 0, 0), ("cm", 1, 0), ("cs", 2, 0), ("cs", 2, 1), ("cm", 1, 1), ("pc", 3, 0),
    ("cm", 2, 0), ("cm", 2, 1), ("pc", 0, 0), ("cs", 3, 0), ("cs", 3, 1), ("cm", 3, 0), ("cs", 0, 0),
    ("dh", 2, 0), ("cs", 0, 1), ("dh", 1, 1), ("cm", 0, 0), ("dh", 3, 0), ("cm", 3, 1), ("dh", 1, 0),
    ("dh", 2, 1), ("cm", 0, 1), ("dh", 0, 0), ("ta", 0, 0), ("b1", 0, 0), ("b1", 1, 0), ("dh", 0, 1),
    ("dh", 3, 1), ("ta", 0, 1), ("b1", 0, 1), ("b1", 1, 1), ("b2", 0, 0), ("bm", 0, 0), ("b2", 0, 1),
    ("bm", 0, 1), ("b2", 1, 1), ("b2", 1, 0), ("bm", 1, 1), ("bm", 1, 0), ("br", 0, 0), ("br", 1, 0),
    ("pb", 0, 0), ("pb", 1, 0), ("dx", 0, 0), ("dx", 1, 0), ("dc", 0, 0), ("pd", 0, 0), ("dc", 1, 0),
    ("pd", 1, 0), ("tz", 0, 0), ("tz", 1, 0),
)


class Names:
    def __init__(self):
        self.names, self.shapes = [], []

    def add(self, name, shape):
        self.names.append(name)
        self.shapes.append(shape)

    def bind(self, refs):
        for name, ref in zip(self.names, refs, strict=True):
            setattr(self, name, ref)


def dot(left, right):
    return jnp.dot(left, right, preferred_element_type=F32)


def dot_last(left, right):
    return lax.dot_general(left, right, (((1,), (1,)), ((), ())), preferred_element_type=F32)


def dot_first(left, right):
    return lax.dot_general(left, right, (((0,), (0,)), ((), ())), preferred_element_type=F32)


def silu_terms(gate_pre):
    sigma = jax.nn.sigmoid(gate_pre)
    silu_val = gate_pre * sigma
    silu_one = sigma * (1.0 + gate_pre * (1.0 - sigma))
    silu_two = sigma * (1.0 - sigma) * (2.0 + gate_pre * (1.0 - 2.0 * sigma))
    return (silu_val, silu_one, silu_two)


def each(lower, upper, body):
    def step(i, carry):
        body(i)
        return carry

    lax.fori_loop(lower, upper, step, 0)


class Exchange:
    def __init__(self, src, dst, sems, n, me, device):
        self.src, self.dst, self.n, self.me, self.device = src, dst, n, me, device
        self.ssem, self.rsem = sems

    def copy(self, k, d, block, landing, device):
        return pltpu.make_async_remote_copy(
            src_ref=self.src.at[k, block],
            dst_ref=self.dst.at[k, landing],
            send_sem=self.ssem.at[k, d],
            recv_sem=self.rsem.at[k, d],
            device_id=device,
            device_id_type=MESH,
        )

    def out(self, k, d):
        to = lax.rem(self.me + d, self.n)
        return self.copy(k, d, to, self.me, self.device(to))

    def start(self, k):
        each(1, self.n, lambda d: self.out(k, d).start())
        self.dst[k, pl.ds(self.me, 1)] = self.src[k, pl.ds(self.me, 1)]

    def wait(self, k):
        def body(d):
            source = lax.rem(self.me + self.n - d, self.n)
            self.copy(k, d, source, source, self.device(source)).wait_recv()

        each(1, self.n, body)

    def drain(self, k):
        each(1, self.n, lambda d: self.out(k, d).wait_send())


class SpreadY(Exchange):
    def __init__(self, ref, core, sems, n, me, device):
        super().__init__(ref, ref, sems, n, me, device)
        self.core = core

    def copy(self, k, d, block, landing, device):
        ref = self.src.at[k, self.core, block]
        return pltpu.make_async_remote_copy(
            src_ref=ref,
            dst_ref=ref,
            send_sem=self.ssem.at[k, d],
            recv_sem=self.rsem.at[k, d],
            device_id=device,
            device_id_type=MESH,
        )

    def out(self, k, d):
        to = lax.rem(self.me + d, self.n)
        return self.copy(k, d, self.me, self.me, self.device(to))

    def start(self, k):
        each(1, self.n, lambda d: self.out(k, d).start())


class Ring:
    def __init__(self):
        self.expert = lax.axis_index("expert")
        self.me = lax.axis_index("mp")
        self.right = lax.rem(self.me + 1, N_MP)
        self.left = lax.rem(self.me + N_MP - 1, N_MP)
        self.opp = lax.rem(self.me + 2, N_MP)

    def copy(self, src, dst, ssem, rsem, to):
        return pltpu.make_async_remote_copy(
            src_ref=src,
            dst_ref=dst,
            send_sem=ssem,
            recv_sem=rsem,
            device_id=(self.expert, to),
            device_id_type=MESH,
        )


class Scatter:
    def __init__(self, ring, part, hop, total, sems, rows, parts):
        self.ring, self.part, self.hop, self.total = ring, part, hop, total
        self.rows, self.parts = rows // parts, parts
        self.half = self.rows // 2
        self.ssem, self.rsem = sems

    def halves(self, b):
        return pl.ds(b * self.rows, self.half), pl.ds(b * self.rows + self.half, self.half)

    def copy(self, k, b, i):
        r, j = self.ring, k * self.parts + b
        first, second = self.halves(b)
        part, hop, total = self.part.at[k], self.hop.at[j], self.total.at[k]
        plan = (
            (part.at[r.opp, first], hop.at[0], r.left),
            (part.at[r.opp, second], hop.at[1], r.right),
            (part.at[r.left, second], total.at[0, second], r.left),
            (part.at[r.right, first], total.at[1, first], r.right),
            (part.at[r.left, first], total.at[0, first], r.left),
            (part.at[r.right, second], total.at[1, second], r.right),
        )
        src, dst, to = plan[i]
        return r.copy(src, dst, self.ssem.at[j, i], self.rsem.at[j, i], to)

    def start(self, k, b, index):
        self.copy(k, b, index).start()

    def middle(self, k, b=0):
        r = self.ring
        first, second = self.halves(b)
        self.copy(k, b, 0).wait_recv()
        self.add(k, b, r.left, first, 0)
        self.copy(k, b, 4).start()
        self.copy(k, b, 1).wait_recv()
        self.add(k, b, r.right, second, 1)
        self.copy(k, b, 5).start()

    def add(self, k, b, block, rows, side):
        hop = self.hop[k * self.parts + b, side].astype(F32)
        value = self.part[k, pl.ds(block, 1), rows, :][0].astype(F32) + hop
        self.part[k, pl.ds(block, 1), rows, :] = value.astype(BF)[None]

    def finish(self, k, b=0):
        for i in (2, 3, 4, 5):
            self.copy(k, b, i).wait_recv()
        rows = pl.ds(b * self.rows, self.rows)
        own = self.part[k, pl.ds(self.ring.me, 1), rows, :][0].astype(F32)
        return own + self.total[k, 0, rows, :].astype(F32) + self.total[k, 1, rows, :].astype(F32)

    def drain(self, k):
        for b in range(self.parts):
            for i in range(6):
                self.copy(k, b, i).wait_send()


class Gather:
    def __init__(self, ring, full, sems, rows, parts):
        self.ring, self.full = ring, full
        self.rows, self.parts = rows // parts, parts
        self.half = self.rows // 2
        self.ssem, self.rsem = sems

    def move(self, k, b, i, block, side, to):
        ref = self.full.at[k, block, pl.ds(b * self.rows + side * self.half, self.half)]
        j = k * self.parts + b
        return self.ring.copy(ref, ref, self.ssem.at[j, i], self.rsem.at[j, i], to)

    def copy(self, k, b, i):
        r = self.ring
        plan = (
            (r.me, 0, r.left),
            (r.me, 1, r.right),
            (r.me, 1, r.left),
            (r.me, 0, r.right),
            (r.right, 0, r.left),
            (r.left, 1, r.right),
        )
        return self.move(k, b, i, *plan[i])

    def arrival(self, k, b, i):
        r = self.ring
        plan = ((r.right, 0), (r.left, 1), (r.right, 1), (r.left, 0), (r.opp, 0), (r.opp, 1))
        return self.move(k, b, i, *plan[i], r.left)

    def start(self, k, b=0):
        for i in range(4):
            self.copy(k, b, i).start()

    def middle(self, k, b=0):
        for i in range(2):
            self.arrival(k, b, i).wait_recv()
            self.copy(k, b, 4 + i).start()

    def finish(self, k, b=0):
        for i in range(2, 6):
            self.arrival(k, b, i).wait_recv()

    def drain(self, k):
        for b in range(self.parts):
            for i in range(6):
                self.copy(k, b, i).wait_send()


def iota(shape, dim):
    return lax.broadcasted_iota(jnp.int32, shape, dim)


def kernel(sizes, names, *refs):
    attn_h, out_proj_h, tan_proj_h, resid, target, routes, gates, w_gate_h, w_up_h, w_down_h, out = refs[:11]
    s = names
    s.bind(refs[11:])
    nz, nyc, cap, tokens, quarter, hidden, chunks, back_chunks = sizes
    ny = nyc // N_CORE
    cw = quarter // chunks
    bw = quarter // 2 // back_chunks
    half = nz * cap
    block = 2 * half
    rows = nyc * block
    model = N_MP * quarter

    ring = Ring()
    me_e, me_m = ring.expert, ring.me
    z, yc = lax.div(me_e, nyc), lax.rem(me_e, nyc)
    y, core = lax.div(yc, N_CORE), lax.rem(yc, N_CORE)

    def at_z(to):
        return (to * nyc + yc, me_m)

    def at_yc(to):
        return (z * nyc + to, me_m)

    loads = [
        pltpu.make_async_copy(src, dst, s.load_sem.at[i])
        for i, (src, dst) in enumerate(
            (
                (attn_h, s.attn),
                (out_proj_h, s.out_proj),
                (tan_proj_h, s.tan_proj),
                (w_gate_h.at[0], s.w_gate),
                (w_up_h.at[0], s.w_up),
                (w_down_h.at[0], s.w_down),
            )
        )
    ]
    for load in loads:
        load.start()

    barrier = pltpu.get_barrier_semaphore()
    counts = {}

    def nth(stage):
        counts[stage] = counts.get(stage, -1) + 1
        return counts[stage]

    def greet(device):
        pl.semaphore_signal(barrier, inc=1, device_id=device, device_id_type=MESH)

    each(1, nz, lambda d: greet(at_z(lax.rem(z + d, nz))))
    each(1, nyc, lambda d: greet(at_yc(lax.rem(yc + d, nyc))))
    each(1, N_MP, lambda d: greet((me_e, lax.rem(me_m + d, N_MP))))

    def sems(name):
        return getattr(s, name + "_ssem"), getattr(s, name + "_rsem")

    scat_z = Scatter(ring, s.part_z, s.hop_z, s.total_z, sems("scat_z"), 2 * tokens, 1)
    go_z = Exchange(s.go_a, s.go_b, sems("go_z"), nz, z, at_z)
    go_yc = Exchange(s.go_c, s.go_d, sems("go_yc"), nyc, yc, at_yc)
    gather_x = Gather(ring, s.x_full, sems("gather_x"), rows, PARTS)
    scat_o = Scatter(ring, s.part_o, s.hop_o, s.total_o, sems("scat_o"), rows, PARTS)
    ret_yc = Exchange(s.ret_a, s.ret_b, sems("ret_yc"), nyc, yc, at_yc)
    ret_z = Exchange(s.ret_c, s.ret_d, sems("ret_z"), nz, z, at_z)
    cot_z = Exchange(s.cot_a, s.cot_b, sems("cot_z"), nz, z, at_z)
    cot_yc = Exchange(s.cot_c, s.cot_d, sems("cot_yc"), nyc, yc, at_yc)
    gather_c = Gather(ring, s.c_full, sems("gather_c"), rows, PARTS)
    scat_b = Scatter(ring, s.part_b, s.hop_b, s.total_b, sems("scat_b"), rows, PARTS)
    bak_yc = Exchange(s.bak_a, s.bak_b, sems("bak_yc"), nyc, yc, at_yc)
    bak_z = Exchange(s.bak_c, s.bak_d, sems("bak_z"), nz, z, at_z)
    att_yc = Exchange(s.att_a, s.att_b, sems("att_yc"), nyc, yc, at_yc)
    gather_a = Gather(ring, s.att_full, sems("gather_a"), quarter, 1)
    spread_y = SpreadY(s.dx, core, sems("spread_y"), ny, y, lambda to: at_yc(to * N_CORE + core))
    ex_z = Exchange(s.sum_z, s.in_z, sems("ex_z"), nz, z, at_z)
    last = Exchange(s.last_a, s.last_b, sems("last"), N_MP, me_m, lambda to: (me_e, to))

    def swap(src, dst, k, width):
        value = dot(s.swap[...], src[k].reshape(rows, width))
        dst[k] = value.astype(BF).reshape(nyc, block, width)

    per = quarter // (nz * nyc)
    run = nz * per
    part_rows, part_blocks = rows // PARTS, nyc // PARTS

    def z_part(k, q):
        columns = pl.ds(pl.multiple_of(q * quarter + k * cw, 128), cw)
        s.part_z[k, pl.ds(q, 1), pl.ds(0, tokens), :] = dot(s.attn[...], s.out_proj[:, columns]).astype(BF)[None]
        s.part_z[k, pl.ds(q, 1), pl.ds(tokens, tokens), :] = dot(s.attn[...], s.tan_proj[:, columns]).astype(BF)[None]

    def z_first(k, _):
        scat_z.start(k, 0, 0)
        scat_z.start(k, 0, 1)

    def z_second(k, _):
        scat_z.start(k, 0, 2)
        scat_z.start(k, 0, 3)
        if nth("z_second") == chunks - 1:
            att_yc.start(0)

    def route_rows():
        eye = iota((tokens, tokens), 0) == iota((tokens, tokens), 1)
        earlier_row = (iota((tokens, tokens), 1) < iota((tokens, tokens), 0)).astype(F32)
        earlier_column = (iota((tokens, tokens), 0) < iota((tokens, tokens), 1)).astype(F32)

        def column(row, zero):
            return jnp.sum(jnp.where(eye, row, zero), axis=1, keepdims=True)

        first, second = routes[0:1, :], routes[1:2, :]
        gate_rows = gates[0:1, :], gates[1:2, :]
        names_f = [first.astype(F32), second.astype(F32)]
        columns_f = [column(row, 0.0) for row in names_f]
        same = [[(columns_f[i] == names_f[j]).astype(F32) for j in range(2)] for i in range(2)]

        def line_of(name, position):
            wide, narrow = lax.div(name, nyc), lax.rem(name, nyc)
            return wide * block + narrow * cap + position

        place_row = [
            line_of(first, jnp.sum(same[0][0] * earlier_column, axis=0, keepdims=True).astype(jnp.int32)),
            line_of(
                second,
                (
                    jnp.sum(same[0][1], axis=0, keepdims=True)
                    + jnp.sum(same[1][1] * earlier_column, axis=0, keepdims=True)
                ).astype(jnp.int32),
            ),
        ]
        place_column = [
            line_of(
                columns_f[0].astype(jnp.int32),
                jnp.sum(same[0][0] * earlier_row, axis=1, keepdims=True).astype(jnp.int32),
            ),
            line_of(
                columns_f[1].astype(jnp.int32),
                (
                    jnp.sum(same[1][0], axis=1, keepdims=True)
                    + jnp.sum(same[1][1] * earlier_row, axis=1, keepdims=True)
                ).astype(jnp.int32),
            ),
        ]
        across, down = iota((tokens, rows), 1), iota((rows, tokens), 0)
        weight = jnp.zeros((rows, 1), F32)
        for h in range(2):
            at = pl.ds(h * tokens, tokens)
            s.back0[at, :] = (across == place_column[0] + h * half).astype(F32).astype(BF)
            s.back1[at, :] = (across == place_column[1] + h * half).astype(F32).astype(BF)
            hits = [down == place_row[i] + h * half for i in range(2)]
            s.pick[:, at] = (hits[0] | hits[1]).astype(F32).astype(BF)
            chosen = jnp.where(hits[0], gate_rows[0], 0.0) + jnp.where(hits[1], gate_rows[1], 0.0)
            weight = weight + jnp.sum(chosen, axis=1, keepdims=True)
        s.slot_gate[...] = weight
        both = [column(row, 0.0) for row in gate_rows]
        for i in range(2):
            s.gate_column[i] = jnp.concatenate([both[i], both[i]], 0)

    def swap_rows():
        r = iota((rows, 1), 0)
        a, h, b, p = r // block, (r % block) // half, (r % half) // cap, r % cap
        s.swap[...] = (iota((rows, rows), 1) == b * block + h * half + a * cap + p).astype(F32).astype(BF)

    def spread_x(k, _):
        value = scat_z.finish(k)
        columns = pl.ds(k * cw, cw)
        s.x_in[k, pl.ds(0, tokens), :] = (
            resid[:, columns].astype(F32) + value[:tokens]
        ).astype(BF)
        s.x_in[k, pl.ds(tokens, tokens), :] = value[tokens:].astype(BF)
        s.go_a[k] = dot(s.pick[...], s.x_in[k]).astype(BF).reshape(nz, block, cw)
        go_z.start(k)
        if nth("spread_x") == chunks - 1:
            att_yc.wait(0)
            s.att_full[0, pl.ds(me_m, 1)] = s.att_b[0].reshape(1, nyc * run, tokens)
            gather_a.start(0)

    def pass_x(k, _):
        go_z.wait(k)
        swap(s.go_b, s.go_c, k, cw)
        go_yc.start(k)
        if nth("pass_x") == chunks - 1:
            gather_a.middle(0)

    def gather_start_x(k, b):
        if b == 0:
            go_yc.wait(k)
            s.x_full[k, pl.ds(me_m, 1)] = s.go_d[k].reshape(1, rows, cw)
        gather_x.start(k, b)

    step_rows = 2 * block

    def pre_acts(k, b):
        gather_x.finish(k, b)
        before = nth(("pre_acts", b))
        if nth("pre_acts") == 0:
            loads[3].wait()
            loads[4].wait()

        def body(i):
            at = pl.ds(pl.multiple_of(b * part_rows + i * step_rows, step_rows), step_rows)
            gate = jnp.zeros((step_rows, hidden), F32)
            up = jnp.zeros((step_rows, hidden), F32)
            for m in range(N_MP):
                features = pl.ds(m * quarter + k * cw, cw)
                values = s.x_full[k, m, at, :]
                gate = gate + dot_last(values, s.w_gate[:, features])
                up = up + dot_last(values, s.w_up[:, features])
            if before:
                gate = gate + s.gate[at, :]
                up = up + s.up[at, :]
            s.gate[at, :] = gate
            s.up[at, :] = up

        each(0, part_rows // step_rows, body)

    def attn_blocks():
        r = iota((quarter, 1), 0)
        c, zz, p = r // run, (r % run) // per, r % per
        wanted = (zz * nyc + c) * per + p
        permute = (iota((quarter, quarter), 1) == wanted).astype(F32).astype(BF)
        s.att_a[0] = dot_last(permute, s.attn[...]).astype(BF).reshape(nyc, run, tokens)

    def activations(i):
        at, tan_at = pl.ds(pl.multiple_of(i * block, 8), half), pl.ds(pl.multiple_of(i * block + half, 8), half)
        gate_pre, gate_tan = s.gate[at, :], s.gate[tan_at, :]
        up_pre, up_tan = s.up[at, :], s.up[tan_at, :]
        silu_val, silu_one, _ = silu_terms(gate_pre)
        hid = silu_val * up_pre
        hid_tan = silu_one * gate_tan * up_pre + silu_val * up_tan
        s.hidden[pl.ds(pl.multiple_of(i * block, 16), block), :] = jnp.concatenate([hid, hid_tan], 0).astype(BF)

    def hidden_units(_, b):
        each(b * part_blocks, (b + 1) * part_blocks, activations)
        if nth("hidden_units") == 0:
            loads[5].wait()

    def o_part(k, b, q):
        columns = pl.ds(pl.multiple_of(q * quarter + k * cw, 128), cw)
        at = pl.ds(b * part_rows, part_rows)
        s.part_o[k, pl.ds(q, 1), at, :] = dot(s.hidden[at, :], s.w_down[:, columns]).astype(BF)[None]

    def o_first(k, b):
        o_part(k, b, ring.opp)
        scat_o.start(k, b, 0)
        scat_o.start(k, b, 1)

    def o_second(k, b):
        o_part(k, b, ring.left)
        scat_o.start(k, b, 2)
        o_part(k, b, ring.right)
        scat_o.start(k, b, 3)
        o_part(k, b, ring.me)

    def return_o(k, _):
        for b in range(PARTS):
            value = scat_o.finish(k, b).astype(BF)
            s.ret_a[k, pl.ds(b * part_blocks, part_blocks)] = value.reshape(part_blocks, block, cw)
        ret_yc.start(k)

    def pass_o(k, _):
        ret_yc.wait(k)
        swap(s.ret_b, s.ret_c, k, cw)
        ret_z.start(k)

    def combine(values):
        return s.gate_column[0] * dot(s.back0[...], values) + s.gate_column[1] * dot(s.back1[...], values)

    def residual(k, _):
        ret_z.wait(k)
        columns = pl.ds(k * cw, cw)
        both = s.x_in[k].astype(F32) + combine(s.ret_d[k].reshape(rows, cw))
        s.y_tan[:, columns] = both[tokens:]
        diff = both[:tokens] - target[:, columns].astype(F32)
        sent = jnp.concatenate([diff, both[tokens:]], 0).astype(BF)
        s.cot_a[k] = (dot(s.pick[...], sent) * s.slot_gate[...]).astype(BF).reshape(nz, block, cw)
        cot_z.start(k)

    def pass_c(k, _):
        cot_z.wait(k)
        swap(s.cot_b, s.cot_c, k, cw)
        cot_yc.start(k)

    def gather_start_c(k, b):
        if b == 0:
            cot_yc.wait(k)
            s.c_full[k, pl.ds(me_m, 1)] = s.cot_d[k].reshape(1, rows, cw)
        gather_c.start(k, b)

    def grad_hidden(k, b):
        gather_c.finish(k, b)
        before = nth(("grad_hidden", b))

        def body(i):
            at = pl.ds(pl.multiple_of(b * part_rows + i * step_rows, step_rows), step_rows)
            grad = jnp.zeros((step_rows, hidden), F32)
            for m in range(N_MP):
                features = pl.ds(m * quarter + k * cw, cw)
                grad = grad + dot_last(s.c_full[k, m, at, :], s.w_down[:, features])
            if before:
                grad = grad + s.grad[at, :]
            s.grad[at, :] = grad

        each(0, part_rows // step_rows, body)

    def tangents(i):
        at, tan_at = pl.ds(pl.multiple_of(i * block, 8), half), pl.ds(pl.multiple_of(i * block + half, 8), half)
        gate_pre, gate_tan = s.gate[at, :], s.gate[tan_at, :]
        up_pre, up_tan = s.up[at, :], s.up[tan_at, :]
        dh, dh_tan = s.grad[at, :], s.grad[tan_at, :]
        silu_val, silu_one, silu_two = silu_terms(gate_pre)
        da_tan = (dh_tan * up_pre + dh * up_tan) * silu_one + dh * up_pre * silu_two * gate_tan
        db_tan = dh_tan * silu_val + dh * silu_one * gate_tan
        to = pl.ds(pl.multiple_of(i * half, 8), half)
        s.da_tan[to, :] = da_tan
        s.db_tan[to, :] = db_tan

    def tangent_units(_, b):
        each(b * part_blocks, (b + 1) * part_blocks, tangents)

    def b_part(k, b, q):
        at = pl.ds(b * part_rows // 2, part_rows // 2)
        da_tan, db_tan = s.da_tan[at, :].astype(BF), s.db_tan[at, :].astype(BF)
        sides = []
        for h in range(2):
            features = pl.ds(pl.multiple_of(q * quarter + h * (quarter // 2) + k * bw, 128), bw)
            term = dot(da_tan, s.w_gate[:, features]) + dot(db_tan, s.w_up[:, features])
            sides.append(term.reshape(part_blocks, half, bw))
        value = jnp.concatenate(sides, 1).astype(BF).reshape(1, part_rows, bw)
        s.part_b[k, pl.ds(q, 1), pl.ds(b * part_rows, part_rows), :] = value

    def b_first(k, b):
        b_part(k, b, ring.opp)
        scat_b.start(k, b, 0)
        scat_b.start(k, b, 1)

    def b_second(k, b):
        b_part(k, b, ring.left)
        scat_b.start(k, b, 2)
        b_part(k, b, ring.right)
        scat_b.start(k, b, 3)
        b_part(k, b, ring.me)

    def return_b(k, _):
        for b in range(PARTS):
            value = scat_b.finish(k, b).astype(BF)
            s.bak_a[k, pl.ds(b * part_blocks, part_blocks)] = value.reshape(part_blocks, block, bw)
        bak_yc.start(k)

    def pass_b(k, _):
        bak_yc.wait(k)
        swap(s.bak_b, s.bak_c, k, bw)
        bak_z.start(k)

    def grad_in(k, _):
        bak_z.wait(k)
        both = combine(s.bak_d[k].reshape(rows, bw))
        for h in range(2):
            columns = pl.ds(h * (quarter // 2) + k * bw, bw)
            value = (s.y_tan[:, columns] + both[h * tokens : (h + 1) * tokens]).astype(BF)
            s.dx[k, pl.ds(core, 1), pl.ds(y, 1), :, pl.ds(h * bw, bw)] = value.reshape(1, 1, tokens, bw)
        spread_y.start(k)

    other = 1 - core

    def core_copy(k, side):
        return pltpu.make_async_remote_copy(
            src_ref=s.dx.at[k, side],
            dst_ref=s.dx.at[k, side],
            send_sem=s.core_ssem.at[k],
            recv_sem=s.core_rsem.at[k],
            device_id=at_yc(y * N_CORE + other),
            device_id_type=MESH,
        )

    def dx_core(k, _):
        spread_y.wait(k)
        core_copy(k, core).start()

    def attn_rows():
        gather_a.finish(0)
        for c in range(N_CORE):
            for yy in range(ny):
                columns = pl.ds((c * ny + yy) * tokens, tokens)
                for m in range(N_MP):
                    source = pl.ds((yy * N_CORE + c) * run, run)
                    s.att_rows[pl.ds(m * run, run), columns] = s.att_full[0, m, source, :]

    def product(k, _):
        if nth("product") == 0:
            attn_rows()
        core_copy(k, other).wait_recv()
        value = dot(s.att_rows[...], s.dx[k].reshape(nyc * tokens, 2 * bw))
        value = value.reshape(N_MP, nz, per, 2 * bw)
        value = jnp.stack([value[m] for m in range(N_MP)], 1)
        s.sum_z[k] = value.reshape(nz, N_MP * per, 2 * bw).astype(BF)
        ex_z.start(k)

    def total_z(k, _):
        ex_z.wait(k)
        total = jnp.sum(s.in_z[k].astype(F32), axis=0) * (1.0 / math.sqrt(tokens * nz * nyc))
        total = total.reshape(N_MP, per, 2 * bw)
        for h in range(2):
            columns = pl.ds(h * (quarter // 2) + k * bw, bw)
            s.last_a[0, :, :, columns] = total[:, :, h * bw : (h + 1) * bw]

    route_rows()
    swap_rows()
    loads[0].wait()
    attn_blocks()
    loads[1].wait()
    loads[2].wait()
    for k in range(chunks):
        for q in (ring.opp, ring.left, ring.right, ring.me):
            z_part(k, q)
    pl.semaphore_wait(barrier, nz + nyc + N_MP - 3)
    stages = {
        "z1": z_first,
        "z2": z_second,
        "zm": scat_z.middle,
        "sp": spread_x,
        "pa": pass_x,
        "gs": gather_start_x,
        "gm": gather_x.middle,
        "pr": pre_acts,
        "ac": hidden_units,
        "o1": o_first,
        "o2": o_second,
        "om": scat_o.middle,
        "rt": return_o,
        "po": pass_o,
        "re": residual,
        "pc": pass_c,
        "cs": gather_start_c,
        "cm": gather_c.middle,
        "dh": grad_hidden,
        "ta": tangent_units,
        "b1": b_first,
        "b2": b_second,
        "bm": scat_b.middle,
        "br": return_b,
        "pb": pass_b,
        "dx": grad_in,
        "dc": dx_core,
        "pd": product,
        "tz": total_z,
    }
    for stage, k, b in ORDER:
        stages[stage](k, b)
    last.start(0)
    last.wait(0)
    for m in range(N_MP):
        out[0, :, m * quarter : (m + 1) * quarter] = s.last_b[0, m]

    for k in range(chunks):
        for stage in (scat_z, go_z, go_yc, gather_x, scat_o, ret_yc, ret_z, cot_z, cot_yc, gather_c):
            stage.drain(k)
    for k in range(back_chunks):
        for stage in (scat_b, bak_yc, bak_z, spread_y, ex_z):
            stage.drain(k)
        core_copy(k, core).wait_send()
    att_yc.drain(0)
    gather_a.drain(0)
    last.drain(0)


def scratch(sizes):
    nz, nyc, cap, tokens, quarter, hidden, chunks, back_chunks = sizes
    ny = nyc // N_CORE
    cw, bw = quarter // chunks, quarter // 2 // back_chunks
    block = 2 * nz * cap
    rows = nyc * block
    model = N_MP * quarter
    per = quarter // (nz * nyc)
    names = Names()

    def vmem(name, shape, kind=BF):
        names.add(name, pltpu.VMEM(shape, kind))

    def sems(name, k, n):
        names.add(name + "_ssem", pltpu.SemaphoreType.DMA((k, n)))
        names.add(name + "_rsem", pltpu.SemaphoreType.DMA((k, n)))

    names.add("load_sem", pltpu.SemaphoreType.DMA((6,)))
    vmem("attn", (tokens, quarter))
    vmem("out_proj", (quarter, model))
    vmem("tan_proj", (quarter, model))
    vmem("w_gate", (hidden, model))
    vmem("w_up", (hidden, model))
    vmem("w_down", (hidden, model))
    vmem("swap", (rows, rows))
    for tag, count, height, width in (
        ("z", chunks, 2 * tokens, cw),
        ("o", chunks, rows, cw),
        ("b", back_chunks, rows, bw),
    ):
        vmem("part_" + tag, (count, N_MP, height, width))
        parts = 1 if tag == "z" else PARTS
        vmem("hop_" + tag, (count * parts, 2, height // 2 // parts, width))
        vmem("total_" + tag, (count, 2, height, width))
        sems("scat_" + tag, count * parts, 6)
    for tag, count, width in (("go", chunks, cw), ("ret", chunks, cw), ("cot", chunks, cw), ("bak", back_chunks, bw)):
        for letter in "abcd":
            vmem(f"{tag}_{letter}", (count, nz, block, width))
        sems(tag + "_z", count, nz)
        sems(tag + "_yc", count, nyc)
    for tag in "xc":
        vmem(tag + "_full", (chunks, N_MP, rows, cw))
        sems("gather_" + tag, chunks * PARTS, 6)
    run = nz * per
    for letter in "ab":
        vmem("att_" + letter, (1, nyc, run, tokens))
    sems("att_yc", 1, nyc)
    vmem("att_full", (1, N_MP, nyc * run, tokens))
    sems("gather_a", 1, 6)
    vmem("att_rows", (N_MP * run, nyc * tokens))
    vmem("pick", (rows, 2 * tokens))
    vmem("back0", (2 * tokens, rows))
    vmem("back1", (2 * tokens, rows))
    vmem("slot_gate", (rows, 1), F32)
    vmem("gate_column", (2, 2 * tokens, 1), F32)
    vmem("x_in", (chunks, 2 * tokens, cw))
    vmem("gate", (rows, hidden), F32)
    vmem("up", (rows, hidden), F32)
    vmem("grad", (rows, hidden), F32)
    vmem("hidden", (rows, hidden))
    vmem("da_tan", (rows // 2, hidden), F32)
    vmem("db_tan", (rows // 2, hidden), F32)
    vmem("y_tan", (tokens, quarter), F32)
    vmem("dx", (back_chunks, N_CORE, ny, tokens, 2 * bw))
    sems("spread_y", back_chunks, ny)
    names.add("core_ssem", pltpu.SemaphoreType.DMA((back_chunks,)))
    names.add("core_rsem", pltpu.SemaphoreType.DMA((back_chunks,)))
    vmem("sum_z", (back_chunks, nz, N_MP * per, 2 * bw))
    vmem("in_z", (back_chunks, nz, N_MP * per, 2 * bw))
    sems("ex_z", back_chunks, nz)
    vmem("last_a", (1, N_MP, per, quarter), F32)
    vmem("last_b", (1, N_MP, per, quarter), F32)
    sems("last", 1, N_MP)
    return names


def local(nz, nyc, attn, out_proj, tangent_proj, resid, target, routes, gates, w_gate, w_up, w_down):
    tokens, quarter = attn.shape
    hidden = w_gate.shape[2]
    experts = nz * nyc
    cap = max(2, 5 * 2 * tokens // (4 * experts))
    sizes = (nz, nyc, cap, tokens, quarter, hidden, CHUNKS, BACK_CHUNKS)
    names = scratch(sizes)
    vmem, anywhere = pl.BlockSpec(memory_space=pltpu.VMEM), pl.BlockSpec(memory_space=pl.ANY)
    return pl.pallas_call(
        functools.partial(kernel, sizes, names),
        out_shape=jax.ShapeDtypeStruct((1, quarter // experts, N_MP * quarter), F32),
        in_specs=[anywhere] * 3 + [vmem] * 4 + [anywhere] * 3,
        out_specs=vmem,
        scratch_shapes=names.shapes,
        compiler_params=pltpu.CompilerParams(
            collective_id=0, has_side_effects=True, vmem_limit_bytes=60 * 2**20
        ),
        cost_estimate=pl.CostEstimate(flops=6_000_000_000, bytes_accessed=12_000_000, transcendentals=300_000),
    )(
        attn,
        out_proj,
        tangent_proj,
        resid,
        target,
        routes.T,
        gates.T,
        jnp.swapaxes(w_gate, 1, 2),
        jnp.swapaxes(w_up, 1, 2),
        w_down,
    )


def solution(mesh):
    experts = mesh.shape["expert"]
    nz = 1 << ((experts.bit_length() - 1) // 2)
    in_specs = (
        P("expert", "mp"),
        P("mp", None),
        P("mp", None),
        P("expert", "mp"),
        P("expert", "mp"),
        P("expert", None),
        P("expert", None),
        P("expert", None, "mp"),
        P("expert", None, "mp"),
        P("expert", "mp", None),
    )
    return jax.shard_map(
        functools.partial(local, nz, experts // nz),
        mesh=mesh,
        in_specs=in_specs,
        out_specs=P("mp", "expert", None),
        check_vma=False,
    )
```

```python
import functools
import math

import jax
import jax.numpy as jnp
from jax import lax
from jax.experimental import pallas as pl
from jax.experimental.pallas import tpu as pltpu
from jax.sharding import PartitionSpec as P

MESH = pl.DeviceIdType.MESH
BF = jnp.bfloat16
F32 = jnp.float32
N_MP = 4
N_CORE = 2
CHUNKS = 4
BACK_CHUNKS = 2
PARTS = 2
ORDER = (
    ("z1", 3, 0), ("z1", 1, 0), ("z2", 3, 0), ("z1", 2, 0), ("zm", 3, 0), ("z2", 1, 0), ("zm", 1, 0),
    ("z1", 0, 0), ("z2", 0, 0), ("sp", 3, 0), ("zm", 0, 0), ("sp", 1, 0), ("z2", 2, 0), ("sp", 0, 0),
    ("zm", 2, 0), ("pa", 3, 0), ("sp", 2, 0), ("pa", 1, 0), ("gs", 3, 0), ("gs", 3, 1), ("pa", 0, 0),
    ("gs", 1, 0), ("gs", 1, 1), ("gm", 3, 0), ("pa", 2, 0), ("gs", 0, 0), ("gm", 1, 0), ("gs", 2, 0),
    ("gm", 0, 0), ("gs", 2, 1), ("gm", 2, 0), ("gs", 0, 1), ("gm", 1, 1), ("gm", 3, 1), ("pr", 3, 0),
    ("gm", 2, 1), ("pr", 0, 0), ("pr", 1, 0), ("pr", 2, 0), ("ac", 0, 0), ("gm", 0, 1), ("o1", 1, 0),
    ("o1", 2, 0), ("o2", 1, 0), ("pr", 1, 1), ("pr", 3, 1), ("pr", 2, 1), ("pr", 0, 1), ("ac", 0, 1),
    ("o1", 1, 1), ("om", 1, 0), ("o1", 2, 1), ("o2", 1, 1), ("om", 1, 1), ("o2", 2, 0), ("o2", 2, 1),
    ("om", 2, 1), ("o1", 3, 0), ("om", 2, 0), ("o1", 0, 0), ("o2", 3, 0), ("rt", 1, 0), ("o1", 3, 1),
    ("om", 3, 0), ("rt", 2, 0), ("po", 1, 0), ("o2", 3, 1), ("o2", 0, 0), ("om", 3, 1), ("o1", 0, 1),
    ("po", 2, 0), ("om", 0, 0), ("o2", 0, 1), ("rt", 3, 0), ("om", 0, 1), ("re", 1, 0), ("po", 3, 0),
    ("re", 2, 0), ("rt", 0, 0), ("po", 0, 0), ("pc", 1, 0), ("re", 3, 0), ("pc", 2, 0), ("cs", 1, 0),
    ("cs", 1, 1), ("re", 0, 0), ("cs", 2, 0), ("cs", 2, 1), ("cm", 1, 0), ("pc", 3, 0), ("cm", 2, 0),
    ("cm", 1, 1), ("cm", 2, 1), ("pc", 0, 0), ("cs", 3, 0), ("cs", 3, 1), ("dh", 1, 1), ("dh", 2, 1),
    ("cm", 3, 0), ("cs", 0, 0), ("cs", 0, 1), ("cm", 0, 0), ("cm", 3, 1), ("cm", 0, 1), ("dh", 2, 0),
    ("dh", 1, 0), ("dh", 3, 0), ("dh", 0, 0), ("ta", 0, 0), ("b1", 0, 0), ("dh", 3, 1), ("b1", 1, 0),
    ("dh", 0, 1), ("ta", 0, 1), ("b1", 0, 1), ("b2", 0, 0), ("bm", 0, 0), ("b1", 1, 1), ("b2", 0, 1),
    ("bm", 0, 1), ("b2", 1, 1), ("b2", 1, 0), ("bm", 1, 0), ("bm", 1, 1), ("br", 0, 0), ("br", 1, 0),
    ("pb", 0, 0), ("pb", 1, 0), ("dx", 0, 0), ("dx", 1, 0), ("dc", 0, 0), ("pd", 0, 0), ("dc", 1, 0),
    ("pd", 1, 0), ("tz", 0, 0), ("tz", 1, 0),
)


class Names:
    def __init__(self):
        self.names, self.shapes = [], []

    def add(self, name, shape):
        self.names.append(name)
        self.shapes.append(shape)

    def bind(self, refs):
        for name, ref in zip(self.names, refs, strict=True):
            setattr(self, name, ref)


def dot(left, right):
    return jnp.dot(left, right, preferred_element_type=F32)


def dot_last(left, right):
    return lax.dot_general(left, right, (((1,), (1,)), ((), ())), preferred_element_type=F32)


def dot_first(left, right):
    return lax.dot_general(left, right, (((0,), (0,)), ((), ())), preferred_element_type=F32)


def silu_terms(gate_pre):
    sigma = jax.nn.sigmoid(gate_pre)
    silu_val = gate_pre * sigma
    silu_one = sigma * (1.0 + gate_pre * (1.0 - sigma))
    silu_two = sigma * (1.0 - sigma) * (2.0 + gate_pre * (1.0 - 2.0 * sigma))
    return (silu_val, silu_one, silu_two)


def each(lower, upper, body):
    def step(i, carry):
        body(i)
        return carry

    lax.fori_loop(lower, upper, step, 0)


class Exchange:
    def __init__(self, src, dst, sems, n, me, device):
        self.src, self.dst, self.n, self.me, self.device = src, dst, n, me, device
        self.ssem, self.rsem = sems

    def copy(self, k, d, block, landing, device):
        return pltpu.make_async_remote_copy(
            src_ref=self.src.at[k, block],
            dst_ref=self.dst.at[k, landing],
            send_sem=self.ssem.at[k, d],
            recv_sem=self.rsem.at[k, d],
            device_id=device,
            device_id_type=MESH,
        )

    def out(self, k, d):
        to = lax.rem(self.me + d, self.n)
        return self.copy(k, d, to, self.me, self.device(to))

    def start(self, k):
        each(1, self.n, lambda d: self.out(k, d).start())
        self.dst[k, pl.ds(self.me, 1)] = self.src[k, pl.ds(self.me, 1)]

    def wait(self, k):
        def body(d):
            source = lax.rem(self.me + self.n - d, self.n)
            self.copy(k, d, source, source, self.device(source)).wait_recv()

        each(1, self.n, body)

    def drain(self, k):
        each(1, self.n, lambda d: self.out(k, d).wait_send())


class SpreadY(Exchange):
    def __init__(self, ref, core, sems, n, me, device):
        super().__init__(ref, ref, sems, n, me, device)
        self.core = core

    def copy(self, k, d, block, landing, device):
        ref = self.src.at[k, self.core, block]
        return pltpu.make_async_remote_copy(
            src_ref=ref,
            dst_ref=ref,
            send_sem=self.ssem.at[k, d],
            recv_sem=self.rsem.at[k, d],
            device_id=device,
            device_id_type=MESH,
        )

    def out(self, k, d):
        to = lax.rem(self.me + d, self.n)
        return self.copy(k, d, self.me, self.me, self.device(to))

    def start(self, k):
        each(1, self.n, lambda d: self.out(k, d).start())


class Ring:
    def __init__(self):
        self.expert = lax.axis_index("expert")
        self.me = lax.axis_index("mp")
        self.right = lax.rem(self.me + 1, N_MP)
        self.left = lax.rem(self.me + N_MP - 1, N_MP)
        self.opp = lax.rem(self.me + 2, N_MP)

    def copy(self, src, dst, ssem, rsem, to):
        return pltpu.make_async_remote_copy(
            src_ref=src,
            dst_ref=dst,
            send_sem=ssem,
            recv_sem=rsem,
            device_id=(self.expert, to),
            device_id_type=MESH,
        )


class Scatter:
    def __init__(self, ring, part, hop, total, sems, rows, parts):
        self.ring, self.part, self.hop, self.total = ring, part, hop, total
        self.rows, self.parts = rows // parts, parts
        self.half = self.rows // 2
        self.ssem, self.rsem = sems

    def halves(self, b):
        return pl.ds(b * self.rows, self.half), pl.ds(b * self.rows + self.half, self.half)

    def copy(self, k, b, i):
        r, j = self.ring, k * self.parts + b
        first, second = self.halves(b)
        part, hop, total = self.part.at[k], self.hop.at[j], self.total.at[k]
        plan = (
            (part.at[r.opp, first], hop.at[0], r.left),
            (part.at[r.opp, second], hop.at[1], r.right),
            (part.at[r.left, second], total.at[0, second], r.left),
            (part.at[r.right, first], total.at[1, first], r.right),
            (part.at[r.left, first], total.at[0, first], r.left),
            (part.at[r.right, second], total.at[1, second], r.right),
        )
        src, dst, to = plan[i]
        return r.copy(src, dst, self.ssem.at[j, i], self.rsem.at[j, i], to)

    def start(self, k, b, index):
        self.copy(k, b, index).start()

    def middle(self, k, b=0):
        r = self.ring
        first, second = self.halves(b)
        self.copy(k, b, 0).wait_recv()
        self.add(k, b, r.left, first, 0)
        self.copy(k, b, 4).start()
        self.copy(k, b, 1).wait_recv()
        self.add(k, b, r.right, second, 1)
        self.copy(k, b, 5).start()

    def add(self, k, b, block, rows, side):
        hop = self.hop[k * self.parts + b, side].astype(F32)
        value = self.part[k, pl.ds(block, 1), rows, :][0].astype(F32) + hop
        self.part[k, pl.ds(block, 1), rows, :] = value.astype(BF)[None]

    def finish(self, k, b=0):
        for i in (2, 3, 4, 5):
            self.copy(k, b, i).wait_recv()
        rows = pl.ds(b * self.rows, self.rows)
        own = self.part[k, pl.ds(self.ring.me, 1), rows, :][0].astype(F32)
        return own + self.total[k, 0, rows, :].astype(F32) + self.total[k, 1, rows, :].astype(F32)

    def drain(self, k):
        for b in range(self.parts):
            for i in range(6):
                self.copy(k, b, i).wait_send()


class Gather:
    def __init__(self, ring, full, sems, rows, parts):
        self.ring, self.full = ring, full
        self.rows, self.parts = rows // parts, parts
        self.half = self.rows // 2
        self.ssem, self.rsem = sems

    def move(self, k, b, i, block, side, to):
        ref = self.full.at[k, block, pl.ds(b * self.rows + side * self.half, self.half)]
        j = k * self.parts + b
        return self.ring.copy(ref, ref, self.ssem.at[j, i], self.rsem.at[j, i], to)

    def copy(self, k, b, i):
        r = self.ring
        plan = (
            (r.me, 0, r.left),
            (r.me, 1, r.right),
            (r.me, 1, r.left),
            (r.me, 0, r.right),
            (r.right, 0, r.left),
            (r.left, 1, r.right),
        )
        return self.move(k, b, i, *plan[i])

    def arrival(self, k, b, i):
        r = self.ring
        plan = ((r.right, 0), (r.left, 1), (r.right, 1), (r.left, 0), (r.opp, 0), (r.opp, 1))
        return self.move(k, b, i, *plan[i], r.left)

    def start(self, k, b=0):
        for i in range(4):
            self.copy(k, b, i).start()

    def middle(self, k, b=0):
        for i in range(2):
            self.arrival(k, b, i).wait_recv()
            self.copy(k, b, 4 + i).start()

    def finish(self, k, b=0):
        for i in range(2, 6):
            self.arrival(k, b, i).wait_recv()

    def drain(self, k):
        for b in range(self.parts):
            for i in range(6):
                self.copy(k, b, i).wait_send()


def iota(shape, dim):
    return lax.broadcasted_iota(jnp.int32, shape, dim)


def kernel(sizes, names, *refs):
    attn_h, out_proj_h, tan_proj_h, resid, target, routes, gates, w_gate_h, w_up_h, w_down_h, out = refs[:11]
    s = names
    s.bind(refs[11:])
    nz, nyc, cap, tokens, quarter, hidden, chunks, back_chunks = sizes
    ny = nyc // N_CORE
    cw = quarter // chunks
    bw = quarter // 2 // back_chunks
    half = nz * cap
    block = 2 * half
    rows = nyc * block
    model = N_MP * quarter

    ring = Ring()
    me_e, me_m = ring.expert, ring.me
    z, yc = lax.div(me_e, nyc), lax.rem(me_e, nyc)
    y, core = lax.div(yc, N_CORE), lax.rem(yc, N_CORE)

    def at_z(to):
        return (to * nyc + yc, me_m)

    def at_yc(to):
        return (z * nyc + to, me_m)

    loads = [
        pltpu.make_async_copy(src, dst, s.load_sem.at[i])
        for i, (src, dst) in enumerate(
            (
                (attn_h, s.attn),
                (out_proj_h, s.out_proj),
                (tan_proj_h, s.tan_proj),
                (w_gate_h.at[0], s.w_gate),
                (w_up_h.at[0], s.w_up),
                (w_down_h.at[0], s.w_down),
            )
        )
    ]
    for load in loads:
        load.start()

    barrier = pltpu.get_barrier_semaphore()
    counts = {}

    def nth(stage):
        counts[stage] = counts.get(stage, -1) + 1
        return counts[stage]

    def greet(device):
        pl.semaphore_signal(barrier, inc=1, device_id=device, device_id_type=MESH)

    each(1, nz, lambda d: greet(at_z(lax.rem(z + d, nz))))
    each(1, nyc, lambda d: greet(at_yc(lax.rem(yc + d, nyc))))
    each(1, N_MP, lambda d: greet((me_e, lax.rem(me_m + d, N_MP))))

    def sems(name):
        return getattr(s, name + "_ssem"), getattr(s, name + "_rsem")

    scat_z = Scatter(ring, s.part_z, s.hop_z, s.total_z, sems("scat_z"), 2 * tokens, 1)
    go_z = Exchange(s.go_a, s.go_b, sems("go_z"), nz, z, at_z)
    go_yc = Exchange(s.go_c, s.go_d, sems("go_yc"), nyc, yc, at_yc)
    gather_x = Gather(ring, s.x_full, sems("gather_x"), rows, PARTS)
    scat_o = Scatter(ring, s.part_o, s.hop_o, s.total_o, sems("scat_o"), rows, PARTS)
    ret_yc = Exchange(s.ret_a, s.ret_b, sems("ret_yc"), nyc, yc, at_yc)
    ret_z = Exchange(s.ret_c, s.ret_d, sems("ret_z"), nz, z, at_z)
    cot_z = Exchange(s.cot_a, s.cot_b, sems("cot_z"), nz, z, at_z)
    cot_yc = Exchange(s.cot_c, s.cot_d, sems("cot_yc"), nyc, yc, at_yc)
    gather_c = Gather(ring, s.c_full, sems("gather_c"), rows, PARTS)
    scat_b = Scatter(ring, s.part_b, s.hop_b, s.total_b, sems("scat_b"), rows, PARTS)
    bak_yc = Exchange(s.bak_a, s.bak_b, sems("bak_yc"), nyc, yc, at_yc)
    bak_z = Exchange(s.bak_c, s.bak_d, sems("bak_z"), nz, z, at_z)
    att_yc = Exchange(s.att_a, s.att_b, sems("att_yc"), nyc, yc, at_yc)
    gather_a = Gather(ring, s.att_full, sems("gather_a"), quarter, 1)
    spread_y = SpreadY(s.dx, core, sems("spread_y"), ny, y, lambda to: at_yc(to * N_CORE + core))
    ex_z = Exchange(s.sum_z, s.in_z, sems("ex_z"), nz, z, at_z)
    last = Exchange(s.last_a, s.last_b, sems("last"), N_MP, me_m, lambda to: (me_e, to))

    def drain(count, *stages):
        for k in range(count):
            for stage in stages:
                stage.drain(k)

    def swap(src, dst, k, width):
        value = dot(s.swap[...], src[k].reshape(rows, width))
        dst[k] = value.astype(BF).reshape(nyc, block, width)

    per = quarter // (nz * nyc)
    run = nz * per
    part_rows, part_blocks = rows // PARTS, nyc // PARTS

    def z_part(k, q):
        columns = pl.ds(pl.multiple_of(q * quarter + k * cw, 128), cw)
        s.part_z[k, pl.ds(q, 1), pl.ds(0, tokens), :] = dot(s.attn[...], s.out_proj[:, columns]).astype(BF)[None]
        s.part_z[k, pl.ds(q, 1), pl.ds(tokens, tokens), :] = dot(s.attn[...], s.tan_proj[:, columns]).astype(BF)[None]

    def z_first(k, _):
        scat_z.start(k, 0, 0)
        scat_z.start(k, 0, 1)

    def z_second(k, _):
        scat_z.start(k, 0, 2)
        scat_z.start(k, 0, 3)
        if nth("z_second") == chunks - 1:
            att_yc.start(0)

    def route_rows():
        eye = iota((tokens, tokens), 0) == iota((tokens, tokens), 1)
        earlier_row = (iota((tokens, tokens), 1) < iota((tokens, tokens), 0)).astype(F32)
        earlier_column = (iota((tokens, tokens), 0) < iota((tokens, tokens), 1)).astype(F32)

        def column(row, zero):
            return jnp.sum(jnp.where(eye, row, zero), axis=1, keepdims=True)

        first, second = routes[0:1, :], routes[1:2, :]
        gate_rows = gates[0:1, :], gates[1:2, :]
        names_f = [first.astype(F32), second.astype(F32)]
        columns_f = [column(row, 0.0) for row in names_f]
        same = [[(columns_f[i] == names_f[j]).astype(F32) for j in range(2)] for i in range(2)]

        def line_of(name, position):
            wide, narrow = lax.div(name, nyc), lax.rem(name, nyc)
            return wide * block + narrow * cap + position

        place_row = [
            line_of(first, jnp.sum(same[0][0] * earlier_column, axis=0, keepdims=True).astype(jnp.int32)),
            line_of(
                second,
                (
                    jnp.sum(same[0][1], axis=0, keepdims=True)
                    + jnp.sum(same[1][1] * earlier_column, axis=0, keepdims=True)
                ).astype(jnp.int32),
            ),
        ]
        place_column = [
            line_of(
                columns_f[0].astype(jnp.int32),
                jnp.sum(same[0][0] * earlier_row, axis=1, keepdims=True).astype(jnp.int32),
            ),
            line_of(
                columns_f[1].astype(jnp.int32),
                (
                    jnp.sum(same[1][0], axis=1, keepdims=True)
                    + jnp.sum(same[1][1] * earlier_row, axis=1, keepdims=True)
                ).astype(jnp.int32),
            ),
        ]
        across, down = iota((tokens, rows), 1), iota((rows, tokens), 0)
        weight = jnp.zeros((rows, 1), F32)
        for h in range(2):
            at = pl.ds(h * tokens, tokens)
            s.back0[at, :] = (across == place_column[0] + h * half).astype(F32).astype(BF)
            s.back1[at, :] = (across == place_column[1] + h * half).astype(F32).astype(BF)
            hits = [down == place_row[i] + h * half for i in range(2)]
            s.pick[:, at] = (hits[0] | hits[1]).astype(F32).astype(BF)
            chosen = jnp.where(hits[0], gate_rows[0], 0.0) + jnp.where(hits[1], gate_rows[1], 0.0)
            weight = weight + jnp.sum(chosen, axis=1, keepdims=True)
        s.slot_gate[...] = weight
        both = [column(row, 0.0) for row in gate_rows]
        for i in range(2):
            s.gate_column[i] = jnp.concatenate([both[i], both[i]], 0)

    def swap_rows():
        r = iota((rows, 1), 0)
        a, h, b, p = r // block, (r % block) // half, (r % half) // cap, r % cap
        s.swap[...] = (iota((rows, rows), 1) == b * block + h * half + a * cap + p).astype(F32).astype(BF)

    def spread_x(k, _):
        value = scat_z.finish(k)
        columns = pl.ds(k * cw, cw)
        s.x_in[k, pl.ds(0, tokens), :] = (
            resid[:, columns].astype(F32) + value[:tokens]
        ).astype(BF)
        s.x_in[k, pl.ds(tokens, tokens), :] = value[tokens:].astype(BF)
        s.go_a[k] = dot(s.pick[...], s.x_in[k]).astype(BF).reshape(nz, block, cw)
        go_z.start(k)
        if nth("spread_x") == chunks - 1:
            att_yc.wait(0)
            s.att_full[0, pl.ds(me_m, 1)] = s.att_b[0].reshape(1, nyc * run, tokens)
            gather_a.start(0)

    def pass_x(k, _):
        go_z.wait(k)
        swap(s.go_b, s.go_c, k, cw)
        go_yc.start(k)
        if nth("pass_x") == chunks - 1:
            gather_a.middle(0)

    def gather_start_x(k, b):
        if b == 0:
            go_yc.wait(k)
            s.x_full[k, pl.ds(me_m, 1)] = s.go_d[k].reshape(1, rows, cw)
        gather_x.start(k, b)

    step_rows = 2 * block

    def pre_acts(k, b):
        gather_x.finish(k, b)
        before = nth(("pre_acts", b))
        if nth("pre_acts") == 0:
            loads[3].wait()
            loads[4].wait()

        def body(i):
            at = pl.ds(pl.multiple_of(b * part_rows + i * step_rows, step_rows), step_rows)
            gate = jnp.zeros((step_rows, hidden), F32)
            up = jnp.zeros((step_rows, hidden), F32)
            for m in range(N_MP):
                features = pl.ds(m * quarter + k * cw, cw)
                values = s.x_full[k, m, at, :]
                gate = gate + dot_last(values, s.w_gate[:, features])
                up = up + dot_last(values, s.w_up[:, features])
            if before:
                gate = gate + s.gate[at, :]
                up = up + s.up[at, :]
            s.gate[at, :] = gate
            s.up[at, :] = up

        each(0, part_rows // step_rows, body)

    def attn_blocks():
        r = iota((quarter, 1), 0)
        c, zz, p = r // run, (r % run) // per, r % per
        wanted = (zz * nyc + c) * per + p
        permute = (iota((quarter, quarter), 1) == wanted).astype(F32).astype(BF)
        s.att_a[0] = dot_last(permute, s.attn[...]).astype(BF).reshape(nyc, run, tokens)

    def activations(i):
        at, tan_at = pl.ds(pl.multiple_of(i * block, 8), half), pl.ds(pl.multiple_of(i * block + half, 8), half)
        gate_pre, gate_tan = s.gate[at, :], s.gate[tan_at, :]
        up_pre, up_tan = s.up[at, :], s.up[tan_at, :]
        silu_val, silu_one, _ = silu_terms(gate_pre)
        hid = silu_val * up_pre
        hid_tan = silu_one * gate_tan * up_pre + silu_val * up_tan
        s.hidden[pl.ds(pl.multiple_of(i * block, 16), block), :] = jnp.concatenate([hid, hid_tan], 0).astype(BF)

    def hidden_units(_, b):
        each(b * part_blocks, (b + 1) * part_blocks, activations)
        if nth("hidden_units") == 0:
            loads[5].wait()

    def o_part(k, b, q):
        columns = pl.ds(pl.multiple_of(q * quarter + k * cw, 128), cw)
        at = pl.ds(b * part_rows, part_rows)
        s.part_o[k, pl.ds(q, 1), at, :] = dot(s.hidden[at, :], s.w_down[:, columns]).astype(BF)[None]

    def o_first(k, b):
        o_part(k, b, ring.opp)
        scat_o.start(k, b, 0)
        scat_o.start(k, b, 1)

    def o_second(k, b):
        o_part(k, b, ring.left)
        scat_o.start(k, b, 2)
        o_part(k, b, ring.right)
        scat_o.start(k, b, 3)
        o_part(k, b, ring.me)

    def return_o(k, _):
        for b in range(PARTS):
            value = scat_o.finish(k, b).astype(BF)
            s.ret_a[k, pl.ds(b * part_blocks, part_blocks)] = value.reshape(part_blocks, block, cw)
        ret_yc.start(k)

    def pass_o(k, _):
        ret_yc.wait(k)
        swap(s.ret_b, s.ret_c, k, cw)
        ret_z.start(k)
        if nth("pass_o") == chunks - 1:
            drain(chunks, scat_z, go_z, go_yc, gather_x)

    def combine(values):
        return s.gate_column[0] * dot(s.back0[...], values) + s.gate_column[1] * dot(s.back1[...], values)

    def residual(k, _):
        ret_z.wait(k)
        columns = pl.ds(k * cw, cw)
        both = s.x_in[k].astype(F32) + combine(s.ret_d[k].reshape(rows, cw))
        s.y_tan[:, columns] = both[tokens:]
        diff = both[:tokens] - target[:, columns].astype(F32)
        sent = jnp.concatenate([diff, both[tokens:]], 0).astype(BF)
        s.cot_a[k] = (dot(s.pick[...], sent) * s.slot_gate[...]).astype(BF).reshape(nz, block, cw)
        cot_z.start(k)

    def pass_c(k, _):
        cot_z.wait(k)
        swap(s.cot_b, s.cot_c, k, cw)
        cot_yc.start(k)

    def gather_start_c(k, b):
        if b == 0:
            cot_yc.wait(k)
            s.c_full[k, pl.ds(me_m, 1)] = s.cot_d[k].reshape(1, rows, cw)
        gather_c.start(k, b)

    def grad_hidden(k, b):
        gather_c.finish(k, b)
        before = nth(("grad_hidden", b))

        def body(i):
            at = pl.ds(pl.multiple_of(b * part_rows + i * step_rows, step_rows), step_rows)
            grad = jnp.zeros((step_rows, hidden), F32)
            for m in range(N_MP):
                features = pl.ds(m * quarter + k * cw, cw)
                grad = grad + dot_last(s.c_full[k, m, at, :], s.w_down[:, features])
            if before:
                grad = grad + s.grad[at, :]
            s.grad[at, :] = grad

        each(0, part_rows // step_rows, body)

    def tangents(i):
        at, tan_at = pl.ds(pl.multiple_of(i * block, 8), half), pl.ds(pl.multiple_of(i * block + half, 8), half)
        gate_pre, gate_tan = s.gate[at, :], s.gate[tan_at, :]
        up_pre, up_tan = s.up[at, :], s.up[tan_at, :]
        dh, dh_tan = s.grad[at, :], s.grad[tan_at, :]
        silu_val, silu_one, silu_two = silu_terms(gate_pre)
        da_tan = (dh_tan * up_pre + dh * up_tan) * silu_one + dh * up_pre * silu_two * gate_tan
        db_tan = dh_tan * silu_val + dh * silu_one * gate_tan
        to = pl.ds(pl.multiple_of(i * half, 8), half)
        s.da_tan[to, :] = da_tan
        s.db_tan[to, :] = db_tan

    def tangent_units(_, b):
        each(b * part_blocks, (b + 1) * part_blocks, tangents)

    def b_part(k, b, q):
        at = pl.ds(b * part_rows // 2, part_rows // 2)
        da_tan, db_tan = s.da_tan[at, :].astype(BF), s.db_tan[at, :].astype(BF)
        sides = []
        for h in range(2):
            features = pl.ds(pl.multiple_of(q * quarter + h * (quarter // 2) + k * bw, 128), bw)
            term = dot(da_tan, s.w_gate[:, features]) + dot(db_tan, s.w_up[:, features])
            sides.append(term.reshape(part_blocks, half, bw))
        value = jnp.concatenate(sides, 1).astype(BF).reshape(1, part_rows, bw)
        s.part_b[k, pl.ds(q, 1), pl.ds(b * part_rows, part_rows), :] = value

    def b_first(k, b):
        b_part(k, b, ring.opp)
        scat_b.start(k, b, 0)
        scat_b.start(k, b, 1)

    def b_second(k, b):
        b_part(k, b, ring.left)
        scat_b.start(k, b, 2)
        b_part(k, b, ring.right)
        scat_b.start(k, b, 3)
        b_part(k, b, ring.me)

    def return_b(k, _):
        for b in range(PARTS):
            value = scat_b.finish(k, b).astype(BF)
            s.bak_a[k, pl.ds(b * part_blocks, part_blocks)] = value.reshape(part_blocks, block, bw)
        bak_yc.start(k)

    def pass_b(k, _):
        bak_yc.wait(k)
        swap(s.bak_b, s.bak_c, k, bw)
        bak_z.start(k)
        if nth("pass_b") == back_chunks - 1:
            drain(chunks, scat_o, ret_yc, ret_z, cot_z, cot_yc, gather_c)
            drain(1, att_yc, gather_a)

    def grad_in(k, _):
        bak_z.wait(k)
        both = combine(s.bak_d[k].reshape(rows, bw))
        for h in range(2):
            columns = pl.ds(h * (quarter // 2) + k * bw, bw)
            value = (s.y_tan[:, columns] + both[h * tokens : (h + 1) * tokens]).astype(BF)
            s.dx[k, pl.ds(core, 1), pl.ds(y, 1), :, pl.ds(h * bw, bw)] = value.reshape(1, 1, tokens, bw)
        spread_y.start(k)

    other = 1 - core

    def core_copy(k, side):
        return pltpu.make_async_remote_copy(
            src_ref=s.dx.at[k, side],
            dst_ref=s.dx.at[k, side],
            send_sem=s.core_ssem.at[k],
            recv_sem=s.core_rsem.at[k],
            device_id=at_yc(y * N_CORE + other),
            device_id_type=MESH,
        )

    def dx_core(k, _):
        spread_y.wait(k)
        core_copy(k, core).start()

    def attn_rows():
        gather_a.finish(0)
        for c in range(N_CORE):
            for yy in range(ny):
                columns = pl.ds((c * ny + yy) * tokens, tokens)
                for m in range(N_MP):
                    source = pl.ds((yy * N_CORE + c) * run, run)
                    s.att_rows[pl.ds(m * run, run), columns] = s.att_full[0, m, source, :]

    def product(k, _):
        before = nth("product")
        if before == 0:
            attn_rows()
        core_copy(k, other).wait_recv()
        value = dot(s.att_rows[...], s.dx[k].reshape(nyc * tokens, 2 * bw))
        value = value.reshape(N_MP, nz, per, 2 * bw)
        value = jnp.stack([value[m] for m in range(N_MP)], 1)
        s.sum_z[k] = value.reshape(nz, N_MP * per, 2 * bw).astype(BF)
        ex_z.start(k)
        if before == back_chunks - 1:
            drain(back_chunks, scat_b, bak_yc, bak_z)

    def total_z(k, _):
        ex_z.wait(k)
        total = jnp.sum(s.in_z[k].astype(F32), axis=0) * (1.0 / math.sqrt(tokens * nz * nyc))
        total = total.reshape(N_MP, per, 2 * bw)
        for h in range(2):
            columns = pl.ds(h * (quarter // 2) + k * bw, bw)
            s.last_a[0, :, :, columns] = total[:, :, h * bw : (h + 1) * bw]

    route_rows()
    swap_rows()
    loads[0].wait()
    attn_blocks()
    loads[1].wait()
    loads[2].wait()
    for k in range(chunks):
        for q in (ring.opp, ring.left, ring.right, ring.me):
            z_part(k, q)
    pl.semaphore_wait(barrier, nz + nyc + N_MP - 3)
    stages = {
        "z1": z_first,
        "z2": z_second,
        "zm": scat_z.middle,
        "sp": spread_x,
        "pa": pass_x,
        "gs": gather_start_x,
        "gm": gather_x.middle,
        "pr": pre_acts,
        "ac": hidden_units,
        "o1": o_first,
        "o2": o_second,
        "om": scat_o.middle,
        "rt": return_o,
        "po": pass_o,
        "re": residual,
        "pc": pass_c,
        "cs": gather_start_c,
        "cm": gather_c.middle,
        "dh": grad_hidden,
        "ta": tangent_units,
        "b1": b_first,
        "b2": b_second,
        "bm": scat_b.middle,
        "br": return_b,
        "pb": pass_b,
        "dx": grad_in,
        "dc": dx_core,
        "pd": product,
        "tz": total_z,
    }
    for stage, k, b in ORDER:
        stages[stage](k, b)
    last.start(0)
    last.wait(0)
    for m in range(N_MP):
        out[0, :, m * quarter : (m + 1) * quarter] = s.last_b[0, m]

    drain(back_chunks, spread_y, ex_z)
    for k in range(back_chunks):
        core_copy(k, core).wait_send()
    last.drain(0)


def scratch(sizes):
    nz, nyc, cap, tokens, quarter, hidden, chunks, back_chunks = sizes
    ny = nyc // N_CORE
    cw, bw = quarter // chunks, quarter // 2 // back_chunks
    block = 2 * nz * cap
    rows = nyc * block
    model = N_MP * quarter
    per = quarter // (nz * nyc)
    names = Names()

    def vmem(name, shape, kind=BF):
        names.add(name, pltpu.VMEM(shape, kind))

    def sems(name, k, n):
        names.add(name + "_ssem", pltpu.SemaphoreType.DMA((k, n)))
        names.add(name + "_rsem", pltpu.SemaphoreType.DMA((k, n)))

    names.add("load_sem", pltpu.SemaphoreType.DMA((6,)))
    vmem("attn", (tokens, quarter))
    vmem("out_proj", (quarter, model))
    vmem("tan_proj", (quarter, model))
    vmem("w_gate", (hidden, model))
    vmem("w_up", (hidden, model))
    vmem("w_down", (hidden, model))
    vmem("swap", (rows, rows))
    for tag, count, height, width in (
        ("z", chunks, 2 * tokens, cw),
        ("o", chunks, rows, cw),
        ("b", back_chunks, rows, bw),
    ):
        vmem("part_" + tag, (count, N_MP, height, width))
        parts = 1 if tag == "z" else PARTS
        vmem("hop_" + tag, (count * parts, 2, height // 2 // parts, width))
        vmem("total_" + tag, (count, 2, height, width))
        sems("scat_" + tag, count * parts, 6)
    for tag, count, width in (("go", chunks, cw), ("ret", chunks, cw), ("cot", chunks, cw), ("bak", back_chunks, bw)):
        for letter in "abcd":
            vmem(f"{tag}_{letter}", (count, nz, block, width))
        sems(tag + "_z", count, nz)
        sems(tag + "_yc", count, nyc)
    for tag in "xc":
        vmem(tag + "_full", (chunks, N_MP, rows, cw))
        sems("gather_" + tag, chunks * PARTS, 6)
    run = nz * per
    for letter in "ab":
        vmem("att_" + letter, (1, nyc, run, tokens))
    sems("att_yc", 1, nyc)
    vmem("att_full", (1, N_MP, nyc * run, tokens))
    sems("gather_a", 1, 6)
    vmem("att_rows", (N_MP * run, nyc * tokens))
    vmem("pick", (rows, 2 * tokens))
    vmem("back0", (2 * tokens, rows))
    vmem("back1", (2 * tokens, rows))
    vmem("slot_gate", (rows, 1), F32)
    vmem("gate_column", (2, 2 * tokens, 1), F32)
    vmem("x_in", (chunks, 2 * tokens, cw))
    vmem("gate", (rows, hidden), F32)
    vmem("up", (rows, hidden), F32)
    vmem("grad", (rows, hidden), F32)
    vmem("hidden", (rows, hidden))
    vmem("da_tan", (rows // 2, hidden), F32)
    vmem("db_tan", (rows // 2, hidden), F32)
    vmem("y_tan", (tokens, quarter), F32)
    vmem("dx", (back_chunks, N_CORE, ny, tokens, 2 * bw))
    sems("spread_y", back_chunks, ny)
    names.add("core_ssem", pltpu.SemaphoreType.DMA((back_chunks,)))
    names.add("core_rsem", pltpu.SemaphoreType.DMA((back_chunks,)))
    vmem("sum_z", (back_chunks, nz, N_MP * per, 2 * bw))
    vmem("in_z", (back_chunks, nz, N_MP * per, 2 * bw))
    sems("ex_z", back_chunks, nz)
    vmem("last_a", (1, N_MP, per, quarter), F32)
    vmem("last_b", (1, N_MP, per, quarter), F32)
    sems("last", 1, N_MP)
    return names


def local(nz, nyc, attn, out_proj, tangent_proj, resid, target, routes, gates, w_gate, w_up, w_down):
    tokens, quarter = attn.shape
    hidden = w_gate.shape[2]
    experts = nz * nyc
    cap = max(2, 5 * 2 * tokens // (4 * experts))
    sizes = (nz, nyc, cap, tokens, quarter, hidden, CHUNKS, BACK_CHUNKS)
    names = scratch(sizes)
    vmem, anywhere = pl.BlockSpec(memory_space=pltpu.VMEM), pl.BlockSpec(memory_space=pl.ANY)
    return pl.pallas_call(
        functools.partial(kernel, sizes, names),
        out_shape=jax.ShapeDtypeStruct((1, quarter // experts, N_MP * quarter), F32),
        in_specs=[anywhere] * 3 + [vmem] * 4 + [anywhere] * 3,
        out_specs=vmem,
        scratch_shapes=names.shapes,
        compiler_params=pltpu.CompilerParams(
            collective_id=0, has_side_effects=True, vmem_limit_bytes=60 * 2**20
        ),
        cost_estimate=pl.CostEstimate(flops=6_000_000_000, bytes_accessed=12_000_000, transcendentals=300_000),
    )(
        attn,
        out_proj,
        tangent_proj,
        resid,
        target,
        routes.T,
        gates.T,
        jnp.swapaxes(w_gate, 1, 2),
        jnp.swapaxes(w_up, 1, 2),
        w_down,
    )


def solution(mesh):
    experts = mesh.shape["expert"]
    nz = 1 << ((experts.bit_length() - 1) // 2)
    in_specs = (
        P("expert", "mp"),
        P("mp", None),
        P("mp", None),
        P("expert", "mp"),
        P("expert", "mp"),
        P("expert", None),
        P("expert", None),
        P("expert", None, "mp"),
        P("expert", None, "mp"),
        P("expert", "mp", None),
    )
    return jax.shard_map(
        functools.partial(local, nz, experts // nz),
        mesh=mesh,
        in_specs=in_specs,
        out_specs=P("mp", "expert", None),
        check_vma=False,
    )
```
